128 devices in a mesh: row: 8 (over z, core), col: 16 (over y, x).
Axes of the slice: x: 4, y: 4, z: 4, core: 2. Of those that a mesh axis runs over, the one named last changes fastest.
Arguments:
- hidden_state: bfloat16 [512, 8192], P('col', 'row'), may hold values from -6 to 6
- norm_gain: float32 [8192], P('row'), may hold values from 0.5 to 1.5
- head_weight: bfloat16 [8192, 65536], P('row', 'col'), may hold values from -40 to 40
- targets: int32 [512], replicated, may hold values from 0 to 65535
- gate_act: bfloat16 [512, 26624], P(None, 'col'), may hold values from -6 to 6
- up_act: bfloat16 [512, 26624], P(None, 'col'), may hold values from -6 to 6
Outputs:
- head_grad: bfloat16 [8192, 65536], P('row', 'col')
- grad_hidden: bfloat16 [512, 8192], P('col', 'row')
- down_grad: bfloat16 [26624, 8192], P('col', 'row')
The draws below stay inside these ranges and needn't reach their ends.
All inputs are finite; a program needn't handle non-finite values.
Results may differ from the reference program's by a relative error of at most 0.024.
Values may be sent and summed in bfloat16 or wider, within the bound.
A program may use at most 128 MiB of HBM per device.

```python
import math
import jax
import jax.numpy as jnp
from jax import lax

D = 8192
FF = 26624
V = 65536
TOKENS = 512


def base_hidden(key):
    inner = jax.random.fold_in(key, 11)
    return jnp.clip(jax.random.normal(jax.random.fold_in(inner, 3), (TOKENS, D), jnp.float32), -6.0, 6.0)


def draw_hidden_state(key, part):
    return base_hidden(key).astype(jnp.bfloat16)


def draw_head_weight(key, part):
    inner = jax.random.fold_in(key, 23)
    weights = jax.random.normal(jax.random.fold_in(inner, 1), (D, V), jnp.float32) * (3.0 / jnp.sqrt(float(D)))
    hidden_rows = base_hidden(key)
    chosen_tokens = jax.random.permutation(jax.random.fold_in(inner, 2), TOKENS)[:6]
    chosen_columns = jax.random.permutation(jax.random.fold_in(inner, 3), V)[:12]
    strengths = jnp.array([130.0, 131.5, 210.0, 212.0, 330.0, 332.5, 160.0, 162.0, 260.0, 261.0, 300.0, 302.5], jnp.float32)
    picked = hidden_rows[chosen_tokens[jnp.arange(12) // 2]]
    norms = jnp.sqrt(jnp.mean(picked * picked, axis=1, keepdims=True))
    columns = (picked / norms * strengths[:, None] / D).T
    weights = weights.at[:, chosen_columns].set(columns)
    return jnp.clip(weights, -40.0, 40.0).astype(jnp.bfloat16)


def set_ends(result, own_key, smallest, high):
    longest = result.shape.index(max(result.shape))
    spots = []
    for shift in (0, 1):
        where = [jax.random.randint(jax.random.fold_in(own_key, axis), (), 0, length) for axis, length in enumerate(result.shape)]
        where[longest] = (where[longest] + shift) % result.shape[longest]
        spots.append(tuple(where))
    return result.at[spots[0]].set(smallest).at[spots[1]].set(high)


def level_of(own_key, extent, pieces, least, top_value):
    def one(position, blocks):
        heights = jax.random.uniform(jax.random.fold_in(jax.random.fold_in(own_key, 6), position), (blocks,), jnp.float32, least / len(pieces), top_value / len(pieces))
        return jnp.repeat(jnp.exp(heights), extent[position] // blocks).reshape((-1,) + (1,) * (len(extent) - position - 1))

    gain = one(*pieces[0])
    for cut in pieces[1:]:
        gain = gain * one(*cut)
    return gain


def gaussian(own_key, shape, deviation, limit, cuts=(), kind=jnp.bfloat16):
    gain = level_of(own_key, shape, cuts, -0.22, 0.18) if cuts else 1.0
    result = jax.random.normal(own_key, shape, jnp.float32) * deviation * gain
    return jnp.minimum(jnp.maximum(result, -limit), limit).astype(kind)


def setup_inputs(seed: int = 0) -> dict:
    key_list = jax.random.split(jax.random.key(seed), 7)
    hidden_state = draw_hidden_state(jax.random.fold_in(key_list[6], 71), 0)
    norm_gain = jnp.clip(1.0 + 0.1 * jax.random.normal(key_list[1], (D,), jnp.float32), 0.5, 1.5)
    head_weight = draw_head_weight(jax.random.fold_in(key_list[6], 71), 0)
    targets = set_ends(jax.random.randint(key_list[3], (TOKENS,), 0, V), jax.random.fold_in(key_list[3], 1), 0, V - 1).astype(jnp.int32)
    gate_act = gaussian(key_list[4], (TOKENS, FF), 1.0, 6.0, ((1, 16),))
    up_act = gaussian(key_list[5], (TOKENS, FF), 1.0, 6.0, ((1, 16),))
    return {"hidden_state": hidden_state, "norm_gain": norm_gain, "head_weight": head_weight, "targets": targets, "gate_act": gate_act, "up_act": up_act}


def reference(hidden_state, norm_gain, head_weight, targets, gate_act, up_act):
    widened = hidden_state.astype(jnp.float32)
    scaled = (norm_gain[None, :] * widened).astype(jnp.bfloat16)
    inv_rms = 1.0 / jnp.sqrt(lax.optimization_barrier(jnp.sum(widened * widened, axis=1)) / D + 1e-05)
    logits = inv_rms[:, None] * jnp.dot(scaled, head_weight, preferred_element_type=jnp.float32)
    top_logit = lax.optimization_barrier(jnp.max(logits, axis=1))
    shifted = jnp.exp(logits - top_logit[:, None])
    exp_total = lax.optimization_barrier(jnp.sum(shifted, axis=1))
    moment = lax.optimization_barrier(jnp.sum(shifted * logits, axis=1))
    matches = targets[:, None] == jnp.arange(V, dtype=jnp.int32)[None, :]
    target_logit = lax.optimization_barrier(jnp.sum(jnp.where(matches, logits, 0.0), axis=1))
    scaled_grad = (inv_rms[:, None] * (shifted / exp_total[:, None] - matches.astype(jnp.float32))).astype(jnp.bfloat16)
    curvature = moment / exp_total - target_logit
    block_width = math.gcd(V, 4096)
    grad_blocks = scaled_grad.reshape(TOKENS, V // block_width, block_width).transpose(1, 0, 2)

    def head_block(grad_block):
        return lax.dot_general(scaled, grad_block, (((0,), (0,)), ((), ())), preferred_element_type=jnp.float32).astype(jnp.bfloat16)
    head_grad = lax.map(head_block, grad_blocks).transpose(1, 0, 2).reshape(D, V)
    feature_grad = lax.dot_general(scaled_grad, head_weight, (((1,), (1,)), ((), ())), preferred_element_type=jnp.float32)
    grad_hidden = (norm_gain[None, :] * feature_grad - widened * (inv_rms * inv_rms * curvature)[:, None] / D).astype(jnp.bfloat16)
    activation = (jax.nn.silu(gate_act.astype(jnp.float32)) * up_act.astype(jnp.float32)).astype(jnp.bfloat16)
    down_grad = lax.dot_general(activation, grad_hidden, (((0,), (0,)), ((), ())), preferred_element_type=jnp.float32).astype(jnp.bfloat16)
    return (head_grad, grad_hidden, down_grad)
```

```python
import jax
import jax.numpy as jnp
from jax import lax
from jax.experimental import pallas as pl
from jax.experimental.pallas import tpu as pltpu
from jax.sharding import PartitionSpec as P

D = 8192
EPS = 1e-05
BF, F32, I16, I32 = jnp.bfloat16, jnp.float32, jnp.int16, jnp.int32
MESH = pl.DeviceIdType.MESH
COLS, ROWS = 16, 8
G = 2
SUB = 16
HALF = SUB * COLS
TAIL = 128
CODES = 32000.0
FINE = 64.0
NT = (((1,), (1,)), ((), ()))


def coded(values):
    most = jnp.maximum(jnp.max(jnp.abs(values), axis=1, keepdims=True), 1e-30)
    level = jnp.ceil(jnp.log2(most) * FINE)
    codes = jnp.round(values * (jnp.exp2(level * (-1.0 / FINE)) * CODES))
    return codes.astype(I32).astype(I16), jnp.broadcast_to(level, (values.shape[0], TAIL)).astype(I32).astype(I16)


def decoded(codes, tail):
    level = tail.astype(I32).astype(F32)[:, 0:1]
    return codes.astype(I32).astype(F32) * (jnp.exp2(level * (1.0 / FINE)) * (1.0 / CODES))


def owner_row(q):
    k, ab, b1, b0 = q // 8, (q // 4) % 2, (q // 2) % 2, q % 2
    s_a = jnp.where(ab == 0, b1, b0)
    s_b = jnp.where(ab == 0, b0, b1)
    return (s_b * 2 + (s_a + s_b) % 2) * 2 + k, ab


def kernel(
    hid, gain, tgt, w_hbm,
    own_out, grad_out, scaled_out, all_out,
    w, ag, sq, inv, part, core, m1s, m1r, m2s, m2r, logit, e, grad, st, fac, fg, rsb, gh,
    w_sem, out_sem, ag_s, ag_r, sq_s, sq_r, inv_s, inv_r, c_s, c_r, z1_s, z1_r, z2_s, z2_r,
    e1_s, e1_r, e2_s, e2_r, e3_s, e3_r, st_s, st_r, fa_s, fa_r, rs_s, rs_r, gh_s, gh_r,
):
    row, col = lax.axis_index("row"), lax.axis_index("col")
    z, k = row // 2, row % 2
    hi = z // 2
    s_a = (hi + z) % 2
    s_b = hi
    width = w.shape[1]
    feats = w.shape[0]
    gw = width // G
    dev_core = (z * 2 + (1 - k), col)
    dev_a = ((z + 1 - 2 * (z % 2)) * 2 + k, col)
    dev_b = (((z + 3 + 2 * (z % 2)) % 4) * 2 + k, col)
    first_side = (s_a, s_b)
    second_side = (s_b, s_a)
    first_dev = (dev_a, dev_b)
    second_dev = (dev_b, dev_a)
    keep1 = [k * 128 + ab * 64 + first_side[ab] * 32 for ab in range(2)]
    send1 = [k * 128 + ab * 64 + (1 - first_side[ab]) * 32 for ab in range(2)]
    own = [keep1[ab] + second_side[ab] * 16 for ab in range(2)]
    send2 = [keep1[ab] + (1 - second_side[ab]) * 16 for ab in range(2)]

    def al(v, n=16):
        return pl.multiple_of(v, n)

    def copy(src, dst, ss, rs, dev):
        return pltpu.make_async_remote_copy(
            src_ref=src, dst_ref=dst, send_sem=ss, recv_sem=rs, device_id=dev, device_id_type=MESH
        )

    def col_dev(i):
        return (row, lax.rem(col + i, COLS))

    def row_dev(i):
        return (lax.rem(row + i, ROWS), col)

    def each(n, fn):
        def body(i, carry):
            fn(i)
            return carry

        lax.fori_loop(1, n, body, 0)

    def c_ag(h, i):
        ref = ag.at[h, pl.ds(al(col * SUB), SUB)]
        return copy(ref, ref, ag_s.at[h, i], ag_r.at[h, i], col_dev(i))

    def c_sq(i):
        return copy(sq.at[row], sq.at[row], sq_s.at[i], sq_r.at[i], row_dev(i))

    def c_inv(i):
        return copy(inv.at[col], inv.at[col], inv_s.at[i], inv_r.at[i], col_dev(i))

    def c_core(h, g):
        return copy(part.at[h, g, pl.ds(al((1 - k) * 128), 128)], core.at[h, g], c_s.at[h, g], c_r.at[h, g], dev_core)

    def c_z1(h, g, ab):
        return copy(m1s.at[h, g, ab], m1r.at[h, g, ab], z1_s.at[h, g, ab], z1_r.at[h, g, ab], first_dev[ab])

    def c_z2(h, g, ab):
        return copy(m2s.at[h, g, ab], m2r.at[h, g, ab], z2_s.at[h, g, ab], z2_r.at[h, g, ab], second_dev[ab])

    def c_e1(h, ab):
        ref = e.at[h, pl.ds(al(own[ab]), 16)]
        return copy(ref, ref, e1_s.at[h, ab], e1_r.at[h, ab], second_dev[ab])

    def c_e2(h, ab):
        ref = e.at[h, pl.ds(al(keep1[ab]), 32)]
        return copy(ref, ref, e2_s.at[h, ab], e2_r.at[h, ab], first_dev[ab])

    def c_e3(h):
        ref = e.at[h, pl.ds(al(k * 128), 128)]
        return copy(ref, ref, e3_s.at[h], e3_r.at[h], dev_core)

    def c_st(h, i):
        return copy(st.at[h, col], st.at[h, col], st_s.at[h, i], st_r.at[h, i], col_dev(i))

    def c_fa(h, i):
        return copy(fac.at[h, row], fac.at[h, row], fa_s.at[h, i], fa_r.at[h, i], row_dev(i))

    def c_rs(h, i):
        peer = lax.rem(col + i, COLS)
        return copy(fg.at[h, pl.ds(al(peer * SUB), SUB)], rsb.at[h, col], rs_s.at[h, i], rs_r.at[h, i], col_dev(i))

    def c_gh(h, i):
        ref = gh.at[pl.ds(al(col * 32 + h * SUB), SUB)]
        return copy(ref, ref, gh_s.at[h, i], gh_r.at[h, i], col_dev(i))

    def logits_part(h, g):
        @pl.loop(0, gw // 512)
        def _(n):
            cols = pl.ds(al(n * 512, 512), 512)
            wide = pl.ds(al(g * gw + n * 512, 512), 512)
            part[h, g, :, cols] = jnp.dot(ag[h], w[:, wide], preferred_element_type=F32)

        c_core(h, g).start()

    def reduce_core(h, g):
        c_core(h, g).wait_recv()
        for ab in range(2):
            for s in range(2):
                at = send1[ab] + s * 16
                v = part[h, g, pl.ds(al(at), 16)] + core[h, g, pl.ds(al(at - k * 128), 16)]
                m1s[h, g, ab, s * 16:s * 16 + 16, 0:gw], m1s[h, g, ab, s * 16:s * 16 + 16, gw:] = coded(v)
            c_z1(h, g, ab).start()
        for ab in range(2):
            for s in range(2):
                at = keep1[ab] + s * 16
                part[h, g, pl.ds(al(at), 16)] += core[h, g, pl.ds(al(at - k * 128), 16)]

    def reduce_first(h, g):
        for ab in range(2):
            c_z1(h, g, ab).wait_recv()
            there = pl.ds(al((1 - second_side[ab]) * 16), 16)
            v = part[h, g, pl.ds(al(send2[ab]), 16)] + decoded(m1r[h, g, ab, there, 0:gw], m1r[h, g, ab, there, gw:])
            m2s[h, g, ab, :, 0:gw], m2s[h, g, ab, :, gw:] = coded(v)
            c_z2(h, g, ab).start()
        for ab in range(2):
            here = pl.ds(al(second_side[ab] * 16), 16)
            part[h, g, pl.ds(al(own[ab]), 16)] += decoded(m1r[h, g, ab, here, 0:gw], m1r[h, g, ab, here, gw:])

    def reduce_second(h, g):
        for ab in range(2):
            c_z2(h, g, ab).wait_recv()
            logit[h, ab * 16:ab * 16 + 16, g * gw:(g + 1) * gw] = part[h, g, pl.ds(al(own[ab]), 16)] + decoded(
                m2r[h, g, ab, :, 0:gw], m2r[h, g, ab, :, gw:]
            )

    vocab_start = col * width
    lane = lax.broadcasted_iota(I32, (16, 128), 1)
    cb = min(1024, width)

    def softmax_part(h):
        for ab in range(2):
            rows = slice(ab * 16, ab * 16 + 16)
            q = own[ab] // 16
            inv_col = inv[q, h * 16:h * 16 + 16, 0:1]
            t_col = tgt[h, pl.ds(al(own[ab]), 16), 0:1] - vocab_start
            top = jnp.full((16, 1), -jnp.inf, F32)
            for n in range(width // cb):
                cols = slice(n * cb, (n + 1) * cb)
                x = logit[h, rows, cols] * inv_col
                top = jnp.maximum(top, jnp.max(x, axis=1, keepdims=True))
            total = jnp.zeros((16, 1), F32)
            moment = jnp.zeros((16, 1), F32)
            target = jnp.zeros((16, 1), F32)
            for n in range(width // cb):
                cols = slice(n * cb, (n + 1) * cb)
                x = logit[h, rows, cols] * inv_col
                y = jnp.exp(x - top)
                e[h, pl.ds(al(own[ab]), 16), cols] = y.astype(BF)
                total += jnp.sum(y, axis=1, keepdims=True)
                moment += jnp.sum(y * x, axis=1, keepdims=True)
                ids = lax.broadcasted_iota(I32, (16, cb), 1) + n * cb
                target += jnp.sum(jnp.where(ids == t_col, x, 0.0), axis=1, keepdims=True)
            c_e1(h, ab).start()
            st[h, col, rows, :] = jnp.where(
                lane == 0, top, jnp.where(lane == 1, total, jnp.where(lane == 2, moment, target))
            )
        each(COLS, lambda i: c_st(h, i).start())

    def spread_first(h):
        for ab in range(2):
            c_e1(h, ab).wait_recv()
            c_e2(h, ab).start()

    def spread_second(h):
        for ab in range(2):
            c_e2(h, ab).wait_recv()
        c_e3(h).start()

    def combine(h):
        each(COLS, lambda i: c_st(h, i).wait_recv())
        top = st[h, 0, :, 0:1]
        for j in range(1, COLS):
            top = jnp.maximum(top, st[h, j, :, 0:1])
        total, moment, target = (jnp.zeros((32, 1), F32) for _ in range(3))
        for j in range(COLS):
            s = st[h, j]
            scale = jnp.exp(s[:, 0:1] - top)
            total += s[:, 1:2] * scale
            moment += s[:, 2:3] * scale
            target += s[:, 3:4]
        mine = jnp.exp(st[h, col, :, 0:1] - top) / total
        curv = moment / total - target
        for ab in range(2):
            rows = slice(ab * 16, ab * 16 + 16)
            inv_col = inv[own[ab] // 16, h * 16:h * 16 + 16, 0:1]
            fac[h, row, rows, :] = jnp.where(lane == 0, mine[rows] * inv_col, curv[rows])
        each(ROWS, lambda i: c_fa(h, i).start())

    def gradient(h):
        c_e3(h).wait_recv()
        each(ROWS, lambda i: c_fa(h, i).wait_recv())

        def group(q, carry):
            r, ab = owner_row(q)
            f_col = fac[h, r, pl.ds(al(ab * 16), 16), 0:1]
            inv_col = inv[q, h * 16:h * 16 + 16, 0:1]
            rows = pl.ds(al(q * 16), 16)
            t_col = tgt[h, rows, 0:1] - vocab_start
            for n in range(width // cb):
                cols = slice(n * cb, (n + 1) * cb)
                ids = lax.broadcasted_iota(I32, (16, cb), 1) + n * cb
                y = e[h, rows, cols].astype(F32) * f_col - jnp.where(ids == t_col, inv_col, 0.0)
                grad[h, rows, cols] = y.astype(BF)
            return carry

        lax.fori_loop(0, COLS, group, 0)
        pltpu.make_async_copy(grad.at[h], grad_out.at[h], out_sem.at[h]).start()

        @pl.loop(0, feats // 256)
        def _(n):
            rows = pl.ds(al(n * 256, 256), 256)
            y = lax.dot_general(grad[h], w[rows, :], NT, preferred_element_type=F32)
            fg[h, :, rows] = y.astype(BF)

        each(COLS, lambda i: c_rs(h, i).start())

    def residual(h):
        each(COLS, lambda i: c_rs(h, i).wait_recv())
        total = fg[h, pl.ds(al(col * SUB), SUB), :].astype(F32)

        def add(i, total):
            return total + rsb[h, lax.rem(col + i, COLS)].astype(F32)

        total = lax.fori_loop(1, COLS, add, total)
        r, ab = owner_row(col)
        curv = fac[h, r, pl.ds(al(ab * 16), 16), 1:2]
        inv_col = inv[col, h * 16:h * 16 + 16, 0:1]
        x = hid[h * 16:h * 16 + 16, :].astype(F32)
        y = (gain[...] * total - x * (inv_col * inv_col * curv) / D).astype(BF)
        gh[pl.ds(al(col * 32 + h * SUB), SUB), :] = y
        own_out[h * 16:h * 16 + 16, :] = y
        each(COLS, lambda i: c_gh(h, i).start())

    load = pltpu.make_async_copy(w_hbm, w, w_sem)
    load.start()
    barrier = pltpu.get_barrier_semaphore()
    each(COLS, lambda i: pl.semaphore_signal(barrier, inc=1, device_id=col_dev(i), device_id_type=MESH))
    each(ROWS, lambda i: pl.semaphore_signal(barrier, inc=1, device_id=row_dev(i), device_id_type=MESH))
    for h in range(2):
        x = hid[h * 16:h * 16 + 16, :].astype(F32)
        ag[h, pl.ds(al(col * SUB), SUB), :] = (gain[...] * x).astype(BF)
        sq[row, h * 16:h * 16 + 16, :] = jnp.broadcast_to(jnp.sum(x * x, axis=1, keepdims=True), (16, 128))
    pl.semaphore_wait(barrier, COLS + ROWS - 2)
    each(COLS, lambda i: c_ag(0, i).start())
    each(ROWS, lambda i: c_sq(i).start())
    each(COLS, lambda i: c_ag(1, i).start())
    each(ROWS, lambda i: c_sq(i).wait_recv())
    squares = sq[0]
    for r in range(1, ROWS):
        squares = squares + sq[r]
    inv[col] = 1.0 / jnp.sqrt(squares / D + EPS)
    each(COLS, lambda i: c_inv(i).start())
    load.wait()
    each(COLS, lambda i: c_ag(0, i).wait_recv())
    for g in range(G):
        logits_part(0, g)
    each(COLS, lambda i: c_ag(1, i).wait_recv())
    pltpu.make_async_copy(ag, scaled_out, out_sem.at[2]).start()
    for g in range(G):
        reduce_core(0, g)
        logits_part(1, g)
    for g in range(G):
        reduce_first(0, g)
        reduce_core(1, g)
    each(COLS, lambda i: c_inv(i).wait_recv())
    for g in range(G):
        reduce_second(0, g)
    softmax_part(0)
    for g in range(G):
        reduce_first(1, g)
    spread_first(0)
    for g in range(G):
        reduce_second(1, g)
    softmax_part(1)
    combine(0)
    spread_second(0)
    spread_first(1)
    combine(1)
    gradient(0)
    spread_second(1)
    residual(0)
    gradient(1)
    residual(1)
    for h in range(2):
        each(COLS, lambda i: c_gh(h, i).wait_recv())
    last = pltpu.make_async_copy(gh, all_out, out_sem.at[3])
    last.start()
    each(ROWS, lambda i: c_sq(i).wait_send())
    each(COLS, lambda i: c_inv(i).wait_send())
    for h in range(2):
        each(COLS, lambda i: c_ag(h, i).wait_send())
        each(COLS, lambda i: c_st(h, i).wait_send())
        each(ROWS, lambda i: c_fa(h, i).wait_send())
        each(COLS, lambda i: c_rs(h, i).wait_send())
        each(COLS, lambda i: c_gh(h, i).wait_send())
        for g in range(G):
            c_core(h, g).wait_send()
            for ab in range(2):
                c_z1(h, g, ab).wait_send()
                c_z2(h, g, ab).wait_send()
        for ab in range(2):
            c_e1(h, ab).wait_send()
            c_e2(h, ab).wait_send()
        c_e3(h).wait_send()
        pltpu.make_async_copy(grad.at[h], grad_out.at[h], out_sem.at[h]).wait()
    pltpu.make_async_copy(ag, scaled_out, out_sem.at[2]).wait()
    last.wait()


def on_device(hidden_state, norm_gain, head_weight, targets, gate_act, up_act):
    feats, width = head_weight.shape
    gw = width // G
    tokens = 2 * HALF
    order = targets.reshape(COLS, 2, SUB).transpose(1, 0, 2).reshape(2, HALF, 1)
    order = jnp.broadcast_to(order, (2, HALF, 128))
    vm, hbm = pl.BlockSpec(memory_space=pltpu.VMEM), pl.BlockSpec(memory_space=pl.ANY)
    dma = pltpu.SemaphoreType.DMA

    def pair(*shape):
        return [dma(shape), dma(shape)]

    grad_hidden, grad, scaled, resid = pl.pallas_call(
        kernel,
        out_shape=(
            jax.ShapeDtypeStruct(hidden_state.shape, BF),
            jax.ShapeDtypeStruct((2, HALF, width), BF),
            jax.ShapeDtypeStruct((2, HALF, feats), BF),
            jax.ShapeDtypeStruct((tokens, feats), BF),
        ),
        in_specs=[vm, vm, vm, hbm],
        out_specs=(vm, hbm, hbm, hbm),
        scratch_shapes=[
            pltpu.VMEM((feats, width), BF),
            pltpu.VMEM((2, HALF, feats), BF),
            pltpu.VMEM((ROWS, 32, 128), F32),
            pltpu.VMEM((COLS, 32, 128), F32),
            pltpu.VMEM((2, G, HALF, gw), F32),
            pltpu.VMEM((2, G, HALF // 2, gw), F32),
            pltpu.VMEM((2, G, 2, 32, gw + TAIL), I16),
            pltpu.VMEM((2, G, 2, 32, gw + TAIL), I16),
            pltpu.VMEM((2, G, 2, 16, gw + TAIL), I16),
            pltpu.VMEM((2, G, 2, 16, gw + TAIL), I16),
            pltpu.VMEM((2, 32, width), F32),
            pltpu.VMEM((2, HALF, width), BF),
            pltpu.VMEM((2, HALF, width), BF),
            pltpu.VMEM((2, COLS, 32, 128), F32),
            pltpu.VMEM((2, ROWS, 32, 128), F32),
            pltpu.VMEM((2, HALF, feats), BF),
            pltpu.VMEM((2, COLS, SUB, feats), BF),
            pltpu.VMEM((tokens, feats), BF),
            dma, dma((4,)),
            *pair(2, COLS), *pair(ROWS), *pair(COLS), *pair(2, G), *pair(2, G, 2), *pair(2, G, 2),
            *pair(2, 2), *pair(2, 2), *pair(2), *pair(2, COLS), *pair(2, ROWS), *pair(2, COLS), *pair(2, COLS),
        ],
        compiler_params=pltpu.CompilerParams(
            collective_id=0, has_side_effects=True, vmem_limit_bytes=58 * 2**20
        ),
        name="head_backward",
    )(hidden_state, norm_gain.reshape(1, feats), order, head_weight)
    head_grad = lax.dot_general(
        scaled.reshape(tokens, feats), grad.reshape(tokens, width), (((0,), (0,)), ((), ())),
        preferred_element_type=F32,
    ).astype(BF)
    activation = (jax.nn.silu(gate_act.astype(F32)) * up_act.astype(F32)).astype(BF)
    down_grad = lax.dot_general(
        activation, resid, (((0,), (0,)), ((), ())), preferred_element_type=F32
    ).astype(BF)
    return head_grad, grad_hidden, down_grad


def solution(mesh):
    in_specs = (P("col", "row"), P("row"), P("row", "col"), P(), P(None, "col"), P(None, "col"))
    out_specs = (P("row", "col"), P("col", "row"), P("col", "row"))
    return jax.shard_map(
        on_device, mesh=mesh, in_specs=in_specs, out_specs=out_specs, check_vma=False
    )
```

```python
import jax
import jax.numpy as jnp
from jax import lax
from jax.experimental import pallas as pl
from jax.experimental.pallas import tpu as pltpu
from jax.sharding import PartitionSpec as P

D = 8192
EPS = 1e-05
BF, F32, I16, I32 = jnp.bfloat16, jnp.float32, jnp.int16, jnp.int32
MESH = pl.DeviceIdType.MESH
COLS, ROWS = 16, 8
SIDE = 4
PIECE = 512
G = 2
SUB = 16
HALF = SUB * COLS
TAIL = 128
CODES = 32000.0
FINE = 64.0
STOP = None
NT = (((1,), (1,)), ((), ()))


def coded(values):
    most = jnp.maximum(jnp.max(jnp.abs(values), axis=1, keepdims=True), 1e-30)
    level = jnp.ceil(jnp.log2(most) * FINE)
    codes = jnp.round(values * (jnp.exp2(level * (-1.0 / FINE)) * CODES))
    return codes.astype(I32).astype(I16), jnp.broadcast_to(level, (values.shape[0], TAIL)).astype(I32).astype(I16)


def decoded(codes, tail):
    level = tail.astype(I32).astype(F32)[:, 0:1]
    return codes.astype(I32).astype(F32) * (jnp.exp2(level * (1.0 / FINE)) * (1.0 / CODES))


def owner_row(q):
    k, ab, b1, b0 = q // 8, (q // 4) % 2, (q // 2) % 2, q % 2
    s_a = jnp.where(ab == 0, b1, b0)
    s_b = jnp.where(ab == 0, b0, b1)
    return (s_b * 2 + (s_a + s_b) % 2) * 2 + k, ab


def kernel(
    hid_hbm, gain_hbm, tgt_hbm, w_hbm, gate_hbm, up_hbm,
    own_out, grad_a, grad_b, grad_c, grad_d, scaled_out, all_out, act_out,
    hid, gain, tgt_in, w, gate, up, act, turned, tgt, ag, sq, inv, part, core, m1s, m1r, m2s, m2r, logit, e, grad, st, fac, fg, ra, rb, rc, rd, gh,
    in_sem, out_sem, sq_s, sq_r, inv_s, inv_r, c_s, c_r, z1_s, z1_r, z2_s, z2_r,
    e1_s, e1_r, e2_s, e2_r, e3_s, e3_r, st_s, st_r, fa_s, fa_r,
    aa_s, aa_r, ab_s, ab_r, ac_s, ac_r, ad_s, ad_r, ra_s, ra_r, rb_s, rb_r, rc_s, rc_r, rd_s, rd_r,
    ga_s, ga_r, gb_s, gb_r, gc_s, gc_r, gd_s, gd_r,
):
    row, col = lax.axis_index("row"), lax.axis_index("col")
    z, k = row // 2, row % 2
    hi = z // 2
    s_a = (hi + z) % 2
    s_b = hi
    width = w.shape[1]
    feats = w.shape[0]
    gw = width // G
    hf = feats // 2
    dev_core = (z * 2 + (1 - k), col)
    dev_a = ((z + 1 - 2 * (z % 2)) * 2 + k, col)
    dev_b = (((z + 3 + 2 * (z % 2)) % 4) * 2 + k, col)
    first_side = (s_a, s_b)
    second_side = (s_b, s_a)
    first_dev = (dev_a, dev_b)
    second_dev = (dev_b, dev_a)
    keep1 = [k * 128 + ab * 64 + first_side[ab] * 32 for ab in range(2)]
    send1 = [k * 128 + ab * 64 + (1 - first_side[ab]) * 32 for ab in range(2)]
    own = [keep1[ab] + second_side[ab] * 16 for ab in range(2)]
    send2 = [keep1[ab] + (1 - second_side[ab]) * 16 for ab in range(2)]

    def al(v, n=16):
        return pl.multiple_of(v, n)

    started, coming, stores = [], [], []
    loads = [(w_hbm, w, in_sem.at[0]), (gate_hbm, gate, in_sem.at[1]), (up_hbm, up, in_sem.at[2])]
    loads += [(hid_hbm, hid, in_sem.at[3]), (gain_hbm, gain, in_sem.at[4]), (tgt_hbm, tgt_in, in_sem.at[5])]

    def copy(src, dst, ss, rs, dev):
        return pltpu.make_async_remote_copy(
            src_ref=src, dst_ref=dst, send_sem=ss, recv_sem=rs, device_id=dev, device_id_type=MESH
        )

    def send(make, *key, peers=None):
        started.append((make, key, peers))
        coming.append((make, key, peers))
        if peers:
            each(peers, lambda i: make(*key, i).start())
        else:
            make(*key).start()

    def arrive(make, *key, peers=None):
        coming.remove((make, key, peers))
        if peers:
            each(peers, lambda i: make(*key, i).wait_recv())
        else:
            make(*key).wait_recv()

    def store(src, dst, sem):
        stores.append((src, dst, sem))
        pltpu.make_async_copy(src, dst, sem).start()

    def stored(n):
        src, dst, sem = loads[n]
        del stores[[d is dst for _, d, _ in stores].index(True)]
        pltpu.make_async_copy(src, dst, sem).wait()

    def left(make, key, peers):
        if peers:
            each(peers, lambda i: make(*key, i).wait_send())
        else:
            make(*key).wait_send()

    def col_dev(i):
        return (row, lax.rem(col + i, COLS))

    x, y = col % SIDE, col // SIDE

    def x_dev(i):
        return (row, y * SIDE + lax.rem(x + i, SIDE))

    def y_dev(i):
        return (row, lax.rem(y + i, SIDE) * SIDE + x)

    def row_dev(i):
        return (lax.rem(row + i, ROWS), col)

    def each(n, fn):
        def body(i, carry):
            fn(i)
            return carry

        lax.fori_loop(1, n, body, 0)

    def c_aa(h, i):
        ref = ag.at[h, y, x, :, 0:hf]
        return copy(ref, ref, aa_s.at[h, i], aa_r.at[h, i], x_dev(i))

    def c_ab(h, i):
        ref = ag.at[h, y, x, :, hf:feats]
        return copy(ref, ref, ab_s.at[h, i], ab_r.at[h, i], y_dev(i))

    def c_ac(h, i):
        ref = ag.at[h, y, :, :, 0:hf]
        return copy(ref, ref, ac_s.at[h, i], ac_r.at[h, i], y_dev(i))

    def c_ad(h, i):
        ref = ag.at[h, :, x, :, hf:feats]
        return copy(ref, ref, ad_s.at[h, i], ad_r.at[h, i], x_dev(i))

    def c_sq(i):
        return copy(sq.at[row], sq.at[row], sq_s.at[i], sq_r.at[i], row_dev(i))

    def c_inv(i):
        return copy(inv.at[col], inv.at[col], inv_s.at[i], inv_r.at[i], col_dev(i))

    def c_core(h, g, n):
        cols = pl.ds(al(n * PIECE, PIECE), PIECE)
        return copy(
            part.at[h, g, pl.ds(al((1 - k) * 128), 128), cols], core.at[h, g, :, cols],
            c_s.at[h, g, n], c_r.at[h, g, n], dev_core,
        )

    def c_z1(h, g, ab):
        return copy(m1s.at[h, g, ab], m1r.at[h, g, ab], z1_s.at[h, g, ab], z1_r.at[h, g, ab], first_dev[ab])

    def c_z2(h, g, ab):
        return copy(m2s.at[h, g, ab], m2r.at[h, g, ab], z2_s.at[h, g, ab], z2_r.at[h, g, ab], second_dev[ab])

    def c_e1(h, ab):
        ref = e.at[h, pl.ds(al(own[ab]), 16)]
        return copy(ref, ref, e1_s.at[h, ab], e1_r.at[h, ab], second_dev[ab])

    def c_e2(h, ab):
        ref = e.at[h, pl.ds(al(keep1[ab]), 32)]
        return copy(ref, ref, e2_s.at[h, ab], e2_r.at[h, ab], first_dev[ab])

    def c_e3(h, ab, late):
        ref = e.at[h, pl.ds(al((send1 if late else keep1)[ab]), 32)]
        return copy(ref, ref, e3_s.at[h, ab, late], e3_r.at[h, ab, late], dev_core)

    def c_st(h, i):
        return copy(st.at[h, col], st.at[h, col], st_s.at[h, i], st_r.at[h, i], col_dev(i))

    def c_fa(h, i):
        return copy(fac.at[h, row], fac.at[h, row], fa_s.at[h, i], fa_r.at[h, i], row_dev(i))

    def c_ra(h, i):
        return copy(fg.at[h, :, lax.rem(x + i, SIDE), :, 0:hf], ra.at[h, i], ra_s.at[h, i], ra_r.at[h, i], x_dev(i))

    def c_rb(h, i):
        return copy(fg.at[h, lax.rem(y + i, SIDE), :, :, hf:feats], rb.at[h, i], rb_s.at[h, i], rb_r.at[h, i], y_dev(i))

    def c_rc(h, i):
        return copy(ra.at[h, 0, lax.rem(y + i, SIDE)], rc.at[h, i], rc_s.at[h, i], rc_r.at[h, i], y_dev(i))

    def c_rd(h, i):
        return copy(rb.at[h, 0, lax.rem(x + i, SIDE)], rd.at[h, i], rd_s.at[h, i], rd_r.at[h, i], x_dev(i))

    def c_ga(h, i):
        ref = gh.at[y, x, h, :, 0:hf]
        return copy(ref, ref, ga_s.at[h, i], ga_r.at[h, i], x_dev(i))

    def c_gb(h, i):
        ref = gh.at[y, x, h, :, hf:feats]
        return copy(ref, ref, gb_s.at[h, i], gb_r.at[h, i], y_dev(i))

    def c_gc(h, i):
        ref = gh.at[y, :, h, :, 0:hf]
        return copy(ref, ref, gc_s.at[h, i], gc_r.at[h, i], y_dev(i))

    def c_gd(h, i):
        ref = gh.at[:, x, h, :, hf:feats]
        return copy(ref, ref, gd_s.at[h, i], gd_r.at[h, i], x_dev(i))

    def logits_part(h, g):
        for n in range(gw // PIECE):
            cols = slice(n * PIECE, (n + 1) * PIECE)
            wide = slice(g * gw + n * PIECE, g * gw + (n + 1) * PIECE)
            part[h, g, :, cols] = jnp.dot(ag[h].reshape(HALF, feats), w[:, wide], preferred_element_type=F32)
            send(c_core, h, g, n)

    def reduce_core(h, g):
        for n in range(gw // PIECE):
            arrive(c_core, h, g, n)
        for ab in range(2):
            for s in range(2):
                at = send1[ab] + s * 16
                v = part[h, g, pl.ds(al(at), 16)] + core[h, g, pl.ds(al(at - k * 128), 16)]
                m1s[h, g, ab, s * 16:s * 16 + 16, 0:gw], m1s[h, g, ab, s * 16:s * 16 + 16, gw:] = coded(v)
            send(c_z1, h, g, ab)
        for ab in range(2):
            for s in range(2):
                at = keep1[ab] + s * 16
                part[h, g, pl.ds(al(at), 16)] += core[h, g, pl.ds(al(at - k * 128), 16)]

    def reduce_first(h, g):
        for ab in range(2):
            arrive(c_z1, h, g, ab)
            there = pl.ds(al((1 - second_side[ab]) * 16), 16)
            v = part[h, g, pl.ds(al(send2[ab]), 16)] + decoded(m1r[h, g, ab, there, 0:gw], m1r[h, g, ab, there, gw:])
            m2s[h, g, ab, :, 0:gw], m2s[h, g, ab, :, gw:] = coded(v)
            send(c_z2, h, g, ab)
        for ab in range(2):
            here = pl.ds(al(second_side[ab] * 16), 16)
            part[h, g, pl.ds(al(own[ab]), 16)] += decoded(m1r[h, g, ab, here, 0:gw], m1r[h, g, ab, here, gw:])

    def reduce_second(h, g):
        for ab in range(2):
            arrive(c_z2, h, g, ab)
            logit[h, ab * 16:ab * 16 + 16, g * gw:(g + 1) * gw] = part[h, g, pl.ds(al(own[ab]), 16)] + decoded(
                m2r[h, g, ab, :, 0:gw], m2r[h, g, ab, :, gw:]
            )

    vocab_start = col * width
    lane = lax.broadcasted_iota(I32, (16, 128), 1)
    cb = min(1024, width)

    def softmax_part(h):
        for ab in range(2):
            rows = slice(ab * 16, ab * 16 + 16)
            q = own[ab] // 16
            inv_col = inv[q, h * 16:h * 16 + 16, 0:1]
            t_col = tgt[h, pl.ds(al(own[ab]), 16), 0:1] - vocab_start
            top = jnp.full((16, 1), -jnp.inf, F32)
            for n in range(width // cb):
                cols = slice(n * cb, (n + 1) * cb)
                x = logit[h, rows, cols] * inv_col
                top = jnp.maximum(top, jnp.max(x, axis=1, keepdims=True))
            total = jnp.zeros((16, 1), F32)
            moment = jnp.zeros((16, 1), F32)
            target = jnp.zeros((16, 1), F32)
            for n in range(width // cb):
                cols = slice(n * cb, (n + 1) * cb)
                x = logit[h, rows, cols] * inv_col
                y = jnp.exp(x - top)
                e[h, pl.ds(al(own[ab]), 16), cols] = y.astype(BF)
                total += jnp.sum(y, axis=1, keepdims=True)
                moment += jnp.sum(y * x, axis=1, keepdims=True)
                ids = lax.broadcasted_iota(I32, (16, cb), 1) + n * cb
                target += jnp.sum(jnp.where(ids == t_col, x, 0.0), axis=1, keepdims=True)
            send(c_e1, h, ab)
            st[h, col, rows, :] = jnp.where(
                lane == 0, top, jnp.where(lane == 1, total, jnp.where(lane == 2, moment, target))
            )
        send(c_st, h, peers=COLS)

    def spread_first(h):
        for ab in range(2):
            arrive(c_e1, h, ab)
            send(c_e2, h, ab)
        for ab in range(2):
            send(c_e3, h, ab, 0)

    def spread_second(h):
        for ab in range(2):
            arrive(c_e2, h, ab)
            send(c_e3, h, ab, 1)

    def combine(h):
        arrive(c_st, h, peers=COLS)
        top = st[h, 0, :, 0:1]
        for j in range(1, COLS):
            top = jnp.maximum(top, st[h, j, :, 0:1])
        total, moment, target = (jnp.zeros((32, 1), F32) for _ in range(3))
        for j in range(COLS):
            s = st[h, j]
            scale = jnp.exp(s[:, 0:1] - top)
            total += s[:, 1:2] * scale
            moment += s[:, 2:3] * scale
            target += s[:, 3:4]
        mine = jnp.exp(st[h, col, :, 0:1] - top) / total
        curv = moment / total - target
        for ab in range(2):
            rows = slice(ab * 16, ab * 16 + 16)
            inv_col = inv[own[ab] // 16, h * 16:h * 16 + 16, 0:1]
            fac[h, row, rows, :] = jnp.where(lane == 0, mine[rows] * inv_col, curv[rows])
        send(c_fa, h, peers=ROWS)

    def prepare(h, whose):
        for ab in range(2):
            for late in range(2):
                if whose:
                    arrive(c_e3, h, ab, late)
        if not whose:
            arrive(c_fa, h, peers=ROWS)

        def group(t, carry):
            q = (k + whose - 2 * k * whose) * 8 + t
            r, ab = owner_row(q)
            f_col = fac[h, r, pl.ds(al(ab * 16), 16), 0:1]
            inv_col = inv[q, h * 16:h * 16 + 16, 0:1]
            rows = pl.ds(al(q * 16), 16)
            t_col = tgt[h, rows, 0:1] - vocab_start
            for n in range(width // cb):
                cols = slice(n * cb, (n + 1) * cb)
                ids = lax.broadcasted_iota(I32, (16, cb), 1) + n * cb
                v = e[h, rows, cols].astype(F32) * f_col - jnp.where(ids == t_col, inv_col, 0.0)
                grad[h, rows, cols] = v.astype(BF)
            return carry

        lax.fori_loop(0, 8, group, 0)

    def product(h):
        for n in range(2):
            half = grad.at[h, :, n * width // 2:(n + 1) * width // 2]
            store(half, (grad_a, grad_b, grad_c, grad_d)[2 * h + n], out_sem.at[4 + 2 * h + n])

        for n in range(feats // 256):
            rows = slice(n * 256, (n + 1) * 256)
            v = lax.dot_general(grad[h], w[rows, :], NT, preferred_element_type=F32)
            fg[h, :, :, :, rows] = v.astype(BF).reshape(SIDE, SIDE, SUB, 256)
            if n == feats // 512 - 1:
                send(c_ra, h, peers=SIDE)
        send(c_rb, h, peers=SIDE)

    def sum_first(h):
        arrive(c_ra, h, peers=SIDE)
        total = fg[h, :, x, :, 0:hf].astype(F32)
        for i in range(1, SIDE):
            total = total + ra[h, i].astype(F32)
        ra[h, 0] = total.astype(BF)
        send(c_rc, h, peers=SIDE)
        arrive(c_rb, h, peers=SIDE)
        total = fg[h, y, :, :, hf:feats].astype(F32)
        for i in range(1, SIDE):
            total = total + rb[h, i].astype(F32)
        rb[h, 0] = total.astype(BF)
        send(c_rd, h, peers=SIDE)

    def residual(h):
        r, ab = owner_row(col)
        curv = fac[h, r, pl.ds(al(ab * 16), 16), 1:2]
        inv_col = inv[col, h * 16:h * 16 + 16, 0:1]
        factor = inv_col * inv_col * curv
        for half in range(2):
            cols = slice(half * hf, (half + 1) * hf)
            arrive((c_rc, c_rd)[half], h, peers=SIDE)
            total = (rb[h, 0, x] if half else ra[h, 0, y]).astype(F32)
            for i in range(1, SIDE):
                total = total + (rc, rd)[half][h, i].astype(F32)
            wide = hid[h * 16:h * 16 + 16, cols].astype(F32)
            v = (gain[:, cols] * total - wide * factor / D).astype(BF)
            gh[y, x, h, :, cols] = v
            own_out[h * 16:h * 16 + 16, cols] = v
            send((c_ga, c_gb)[half], h, peers=SIDE)

    def pass_on(h):
        arrive(c_ga, h, peers=SIDE)
        send(c_gc, h, peers=SIDE)
        arrive(c_gb, h, peers=SIDE)
        send(c_gd, h, peers=SIDE)

    def enter():
        for n in range(3, 6):
            store(*loads[n])
        for n in range(3):
            store(*loads[n])
        barrier = pltpu.get_barrier_semaphore()
        each(COLS, lambda i: pl.semaphore_signal(barrier, inc=1, device_id=col_dev(i), device_id_type=MESH))
        each(ROWS, lambda i: pl.semaphore_signal(barrier, inc=1, device_id=row_dev(i), device_id_type=MESH))
        for n in range(3, 6):
            stored(n)
        for h in range(2):
            v = hid[h * 16:h * 16 + 16, :].astype(F32)
            ag[h, y, x] = (gain[...] * v).astype(BF)
            sq[row, h * 16:h * 16 + 16, :] = jnp.broadcast_to(jnp.sum(v * v, axis=1, keepdims=True), (16, 128))
        pl.semaphore_wait(barrier, COLS + ROWS - 2)
        send(c_aa, 0, peers=SIDE)
        send(c_ab, 0, peers=SIDE)
        send(c_sq, peers=ROWS)

    def order_targets():
        ids = jnp.concatenate([tgt_in[...], tgt_in[...]], axis=0).astype(F32).T
        for j in range(COLS):
            for h in range(2):
                at = (j % 4) * 32 + h * 16
                ids_col = ids[at:at + 16, j // 4:j // 4 + 1].astype(I32)
                tgt[h, j * 16:j * 16 + 16, :] = jnp.broadcast_to(ids_col, (16, 128))

    def squares():
        arrive(c_sq, peers=ROWS)
        total = sq[0]
        for r in range(1, ROWS):
            total = total + sq[r]
        inv[col] = 1.0 / jnp.sqrt(total / D + EPS)
        send(c_inv, peers=COLS)

    def activate():
        stored(1)
        stored(2)

        @pl.loop(0, gate.shape[1] // 128)
        def _(n):
            cols = pl.ds(al(n * 128, 128), 128)
            v = gate[:, cols].astype(F32)
            act[cols, :] = (v / (1.0 + jnp.exp(-v)) * up[:, cols].astype(F32)).T.astype(BF)

        store(act, act_out, out_sem.at[1])

    def turn(h):
        at = slice(h * HALF, (h + 1) * HALF)
        for n in range(feats // 256):
            rows = slice(n * 256, (n + 1) * 256)
            turned[rows, at] = ag[h, :, :, :, rows].reshape(HALF, 256).T
        if h == 1:
            store(turned, scaled_out, out_sem.at[2])

    def gather_on(h):
        arrive(c_aa, h, peers=SIDE)
        send(c_ac, h, peers=SIDE)
        arrive(c_ab, h, peers=SIDE)
        send(c_ad, h, peers=SIDE)
        if h == 0:
            send(c_aa, 1, peers=SIDE)
            send(c_ab, 1, peers=SIDE)

    def gathered(h):
        arrive(c_ac, h, peers=SIDE)
        arrive(c_ad, h, peers=SIDE)

    def scales():
        arrive(c_inv, peers=COLS)

    def finish():
        for h in range(2):
            arrive(c_gc, h, peers=SIDE)
            arrive(c_gd, h, peers=SIDE)
        store(gh, all_out, out_sem.at[3])

    steps = [
        (enter,), (gather_on, 0), (order_targets,), (activate,), (stored, 0),
        (gathered, 0), (logits_part, 0, 0), (gather_on, 1), (logits_part, 0, 1), (reduce_core, 0, 0),
        (reduce_core, 0, 1), (squares,), (gathered, 1), (logits_part, 1, 0), (reduce_first, 0, 0), (logits_part, 1, 1),
        (reduce_first, 0, 1), (reduce_core, 1, 0), (reduce_core, 1, 1), (turn, 0), (turn, 1),
        (scales,), (reduce_second, 0, 0), (reduce_second, 0, 1), (softmax_part, 0),
        (reduce_first, 1, 0), (reduce_first, 1, 1), (spread_first, 0),
        (reduce_second, 1, 0), (reduce_second, 1, 1), (softmax_part, 1),
        (combine, 0), (spread_second, 0), (spread_first, 1), (prepare, 0, 0), (prepare, 0, 1), (combine, 1),
        (product, 0), (spread_second, 1), (prepare, 1, 0), (prepare, 1, 1), (product, 1),
        (sum_first, 0), (residual, 0), (sum_first, 1), (pass_on, 0), (residual, 1), (pass_on, 1), (finish,),
    ]
    for step, *which in steps[:STOP]:
        step(*which)
    for make, key, peers in list(coming):
        arrive(make, *key, peers=peers)
    for make, key, peers in started:
        left(make, key, peers)
    for src, dst, sem in stores:
        pltpu.make_async_copy(src, dst, sem).wait()


def weights_kernel(scaled, grad_a, grad_b, grad_c, grad_d, act, resid, head, down):
    i = pl.program_id(0)
    width = head.shape[1]
    at = pl.ds(pl.multiple_of((i % (pl.num_programs(0) // 2)) * width, 128), width)

    def tile(first, second):
        total = jnp.dot(scaled[:, :HALF], first[:, at], preferred_element_type=F32)
        head[...] = (total + jnp.dot(scaled[:, HALF:], second[:, at], preferred_element_type=F32)).astype(BF)

    @pl.when(i < pl.num_programs(0) // 2)
    def _():
        tile(grad_a, grad_c)

    @pl.when(i >= pl.num_programs(0) // 2)
    def _():
        tile(grad_b, grad_d)

    down[...] = jnp.dot(act[...], resid[...], preferred_element_type=F32).astype(BF)


def on_device(hidden_state, norm_gain, head_weight, targets, gate_act, up_act):
    feats, width = head_weight.shape
    gw = width // G
    tokens = 2 * HALF
    hidden_units = gate_act.shape[1]
    vm, hbm = pl.BlockSpec(memory_space=pltpu.VMEM), pl.BlockSpec(memory_space=pl.ANY)
    dma = pltpu.SemaphoreType.DMA

    def pair(*shape):
        return [dma(shape), dma(shape)]

    grad_hidden, *grads, scaled, resid, act = pl.pallas_call(
        kernel,
        out_shape=(
            jax.ShapeDtypeStruct(hidden_state.shape, BF),
            *[jax.ShapeDtypeStruct((HALF, width // 2), BF)] * 4,
            jax.ShapeDtypeStruct((feats, tokens), BF),
            jax.ShapeDtypeStruct((SIDE, SIDE, 2, SUB, feats), BF),
            jax.ShapeDtypeStruct((hidden_units, tokens), BF),
        ),
        in_specs=[pl.BlockSpec(memory_space=pltpu.HBM)] * 6,
        out_specs=(vm, *[hbm] * 7),
        scratch_shapes=[
            pltpu.VMEM(hidden_state.shape, BF),
            pltpu.VMEM((1, feats), F32),
            pltpu.VMEM((4, 128), I32),
            pltpu.VMEM((feats, width), BF),
            pltpu.VMEM((tokens, hidden_units), BF),
            pltpu.VMEM((tokens, hidden_units), BF),
            pltpu.VMEM((hidden_units, tokens), BF),
            pltpu.VMEM((feats, tokens), BF),
            pltpu.VMEM((2, HALF, 128), I32),
            pltpu.VMEM((2, SIDE, SIDE, SUB, feats), BF),
            pltpu.VMEM((ROWS, 32, 128), F32),
            pltpu.VMEM((COLS, 32, 128), F32),
            pltpu.VMEM((2, G, HALF, gw), F32),
            pltpu.VMEM((2, G, HALF // 2, gw), F32),
            pltpu.VMEM((2, G, 2, 32, gw + TAIL), I16),
            pltpu.VMEM((2, G, 2, 32, gw + TAIL), I16),
            pltpu.VMEM((2, G, 2, 16, gw + TAIL), I16),
            pltpu.VMEM((2, G, 2, 16, gw + TAIL), I16),
            pltpu.VMEM((2, 32, width), F32),
            pltpu.VMEM((2, HALF, width), BF),
            pltpu.VMEM((2, HALF, width), BF),
            pltpu.VMEM((2, COLS, 32, 128), F32),
            pltpu.VMEM((2, ROWS, 32, 128), F32),
            pltpu.VMEM((2, SIDE, SIDE, SUB, feats), BF),
            pltpu.VMEM((2, SIDE, SIDE, SUB, feats // 2), BF),
            pltpu.VMEM((2, SIDE, SIDE, SUB, feats // 2), BF),
            pltpu.VMEM((2, SIDE, SUB, feats // 2), BF),
            pltpu.VMEM((2, SIDE, SUB, feats // 2), BF),
            pltpu.VMEM((SIDE, SIDE, 2, SUB, feats), BF),
            dma((6,)), dma((8,)),
            *pair(ROWS), *pair(COLS), *pair(2, G, gw // PIECE), *pair(2, G, 2), *pair(2, G, 2),
            *pair(2, 2), *pair(2, 2), *pair(2, 2, 2), *pair(2, COLS), *pair(2, ROWS),
            *[dma((2, SIDE))] * 24,
        ],
        compiler_params=pltpu.CompilerParams(
            collective_id=0, has_side_effects=True, vmem_limit_bytes=46 * 2**20
        ),
        name="head_backward",
    )(hidden_state, norm_gain.reshape(1, feats), targets.reshape(4, 128), head_weight, gate_act, up_act)
    tiles = 8
    head_grad, down_grad = pl.pallas_call(
        weights_kernel,
        grid=(tiles,),
        out_shape=(
            jax.ShapeDtypeStruct((feats, width), BF),
            jax.ShapeDtypeStruct((hidden_units, feats), BF),
        ),
        in_specs=[vm] * 5 + [pl.BlockSpec((hidden_units // tiles, tokens), lambda i: (i, 0)), vm],
        out_specs=(
            pl.BlockSpec((feats, width // tiles), lambda i: (0, i)),
            pl.BlockSpec((hidden_units // tiles, feats), lambda i: (i, 0)),
        ),
        compiler_params=pltpu.CompilerParams(vmem_limit_bytes=24 * 2**20),
        name="weight_gradients",
    )(scaled, *grads, act, resid.reshape(tokens, feats))
    return head_grad, grad_hidden, down_grad


def solution(mesh):
    in_specs = (P("col", "row"), P("row"), P("row", "col"), P(), P(None, "col"), P(None, "col"))
    out_specs = (P("row", "col"), P("col", "row"), P("col", "row"))
    return jax.shard_map(
        on_device, mesh=mesh, in_specs=in_specs, out_specs=out_specs, check_vma=False
    )
```

```python
import jax
import jax.numpy as jnp
from jax import lax
from jax.experimental import pallas as pl
from jax.experimental.pallas import tpu as pltpu
from jax.sharding import PartitionSpec as P

D = 8192
EPS = 1e-05
BF, F32, I16, I32 = jnp.bfloat16, jnp.float32, jnp.int16, jnp.int32
MESH = pl.DeviceIdType.MESH
COLS, ROWS = 16, 8
SIDE = 4
PIECE = 512
QUARTERS = 4
G = 2
SUB = 16
HALF = SUB * COLS
TAIL = 128
CODES = 32000.0
FINE = 64.0
STOP = None
NT = (((1,), (1,)), ((), ()))


def coded(values):
    most = jnp.maximum(jnp.max(jnp.abs(values), axis=1, keepdims=True), 1e-30)
    level = jnp.ceil(jnp.log2(most) * FINE)
    codes = jnp.round(values * (jnp.exp2(level * (-1.0 / FINE)) * CODES))
    return codes.astype(I32).astype(I16), jnp.broadcast_to(level, (values.shape[0], TAIL)).astype(I32).astype(I16)


def decoded(codes, tail):
    level = tail.astype(I32).astype(F32)[:, 0:1]
    return codes.astype(I32).astype(F32) * (jnp.exp2(level * (1.0 / FINE)) * (1.0 / CODES))


def owner_row(q):
    k, ab, b1, b0 = q // 8, (q // 4) % 2, (q // 2) % 2, q % 2
    s_a = jnp.where(ab == 0, b1, b0)
    s_b = jnp.where(ab == 0, b0, b1)
    return (s_b * 2 + (s_a + s_b) % 2) * 2 + k, ab


def kernel(
    hid_hbm, gain_hbm, tgt_hbm, w_hbm, gate_hbm, up_hbm,
    grad_a, grad_b, grad_c, grad_d, scaled_out, all_out, act_out,
    hid, gain, tgt_in, w, gate, up, act, turned, tgt, ag, sq, inv, part, core, m1s, m1r, m2s, m2r, logit, e, grad, st, fac, fg, ra, rb, rc, rd, gh,
    in_sem, out_sem, sq_s, sq_r, inv_s, inv_r, c_s, c_r, z1_s, z1_r, z2_s, z2_r,
    e1_s, e1_r, e2_s, e2_r, e3_s, e3_r, st_s, st_r, fa_s, fa_r,
    aa_s, aa_r, ab_s, ab_r, ac_s, ac_r, ad_s, ad_r, ra_s, ra_r, rb_s, rb_r, rc_s, rc_r, rd_s, rd_r,
    ga_s, ga_r, gb_s, gb_r, gc_s, gc_r, gd_s, gd_r,
):
    row, col = lax.axis_index("row"), lax.axis_index("col")
    z, k = row // 2, row % 2
    hi = z // 2
    s_a = (hi + z) % 2
    s_b = hi
    width = w.shape[1]
    feats = w.shape[0]
    gw = width // G
    hf = feats // 2
    dev_core = (z * 2 + (1 - k), col)
    dev_a = ((z + 1 - 2 * (z % 2)) * 2 + k, col)
    dev_b = (((z + 3 + 2 * (z % 2)) % 4) * 2 + k, col)
    first_side = (s_a, s_b)
    second_side = (s_b, s_a)
    first_dev = (dev_a, dev_b)
    second_dev = (dev_b, dev_a)
    keep1 = [k * 128 + ab * 64 + first_side[ab] * 32 for ab in range(2)]
    send1 = [k * 128 + ab * 64 + (1 - first_side[ab]) * 32 for ab in range(2)]
    own = [keep1[ab] + second_side[ab] * 16 for ab in range(2)]
    send2 = [keep1[ab] + (1 - second_side[ab]) * 16 for ab in range(2)]

    def al(v, n=16):
        return pl.multiple_of(v, n)

    started, coming, stores = [], [], []
    loads = [(w_hbm, w, in_sem.at[0]), (gate_hbm, gate, in_sem.at[1]), (up_hbm, up, in_sem.at[2])]
    loads += [(hid_hbm, hid, in_sem.at[3]), (gain_hbm, gain, in_sem.at[4]), (tgt_hbm, tgt_in, in_sem.at[5])]

    def copy(src, dst, ss, rs, dev):
        return pltpu.make_async_remote_copy(
            src_ref=src, dst_ref=dst, send_sem=ss, recv_sem=rs, device_id=dev, device_id_type=MESH
        )

    def send(make, *key, peers=None):
        started.append((make, key, peers))
        coming.append((make, key, peers))
        if peers:
            each(peers, lambda i: make(*key, i).start())
        else:
            make(*key).start()

    def arrive(make, *key, peers=None):
        coming.remove((make, key, peers))
        if peers:
            each(peers, lambda i: make(*key, i).wait_recv())
        else:
            make(*key).wait_recv()

    def store(src, dst, sem):
        stores.append((src, dst, sem))
        pltpu.make_async_copy(src, dst, sem).start()

    def stored(n):
        src, dst, sem = loads[n]
        del stores[[d is dst for _, d, _ in stores].index(True)]
        pltpu.make_async_copy(src, dst, sem).wait()

    def left(make, key, peers):
        if peers:
            each(peers, lambda i: make(*key, i).wait_send())
        else:
            make(*key).wait_send()

    def col_dev(i):
        return (row, lax.rem(col + i, COLS))

    x, y = col % SIDE, col // SIDE

    def x_dev(i):
        return (row, y * SIDE + lax.rem(x + i, SIDE))

    def y_dev(i):
        return (row, lax.rem(y + i, SIDE) * SIDE + x)

    def row_dev(i):
        return (lax.rem(row + i, ROWS), col)

    def each(n, fn):
        def body(i, carry):
            fn(i)
            return carry

        lax.fori_loop(1, n, body, 0)

    def c_aa(h, i):
        ref = ag.at[h, y, x, :, 0:hf]
        return copy(ref, ref, aa_s.at[h, i], aa_r.at[h, i], x_dev(i))

    def c_ab(h, i):
        ref = ag.at[h, y, x, :, hf:feats]
        return copy(ref, ref, ab_s.at[h, i], ab_r.at[h, i], y_dev(i))

    def c_ac(h, i):
        ref = ag.at[h, y, :, :, 0:hf]
        return copy(ref, ref, ac_s.at[h, i], ac_r.at[h, i], y_dev(i))

    def c_ad(h, i):
        ref = ag.at[h, :, x, :, hf:feats]
        return copy(ref, ref, ad_s.at[h, i], ad_r.at[h, i], x_dev(i))

    def c_sq(i):
        return copy(sq.at[row], sq.at[row], sq_s.at[i], sq_r.at[i], row_dev(i))

    def c_inv(i):
        return copy(inv.at[col], inv.at[col], inv_s.at[i], inv_r.at[i], col_dev(i))

    def c_core(h, g, n):
        cols = pl.ds(al(n * PIECE, PIECE), PIECE)
        return copy(
            part.at[h, g, pl.ds(al((1 - k) * 128), 128), cols], core.at[h, g, :, cols],
            c_s.at[h, g, n], c_r.at[h, g, n], dev_core,
        )

    def c_z1(h, g, ab):
        return copy(m1s.at[h, g, ab], m1r.at[h, g, ab], z1_s.at[h, g, ab], z1_r.at[h, g, ab], first_dev[ab])

    def c_z2(h, g, ab):
        return copy(m2s.at[h, g, ab], m2r.at[h, g, ab], z2_s.at[h, g, ab], z2_r.at[h, g, ab], second_dev[ab])

    def c_e1(h, ab):
        ref = e.at[h, pl.ds(al(own[ab]), 16)]
        return copy(ref, ref, e1_s.at[h, ab], e1_r.at[h, ab], second_dev[ab])

    def c_e2(h, ab):
        ref = e.at[h, pl.ds(al(keep1[ab]), 32)]
        return copy(ref, ref, e2_s.at[h, ab], e2_r.at[h, ab], first_dev[ab])

    def c_e3(h, ab, late):
        ref = e.at[h, pl.ds(al((send1 if late else keep1)[ab]), 32)]
        return copy(ref, ref, e3_s.at[h, ab, late], e3_r.at[h, ab, late], dev_core)

    def c_st(h, i):
        return copy(st.at[h, col], st.at[h, col], st_s.at[h, i], st_r.at[h, i], col_dev(i))

    def c_fa(h, i):
        return copy(fac.at[h, row], fac.at[h, row], fa_s.at[h, i], fa_r.at[h, i], row_dev(i))

    def c_ra(h, i):
        return copy(fg.at[h, :, lax.rem(x + i, SIDE), :, 0:hf], ra.at[h, i], ra_s.at[h, i], ra_r.at[h, i], x_dev(i))

    def c_rb(h, i):
        return copy(fg.at[h, lax.rem(y + i, SIDE), :, :, hf:feats], rb.at[h, i], rb_s.at[h, i], rb_r.at[h, i], y_dev(i))

    def c_rc(h, i):
        return copy(ra.at[h, 0, lax.rem(y + i, SIDE)], rc.at[h, i], rc_s.at[h, i], rc_r.at[h, i], y_dev(i))

    def c_rd(h, i):
        return copy(rb.at[h, 0, lax.rem(x + i, SIDE)], rd.at[h, i], rd_s.at[h, i], rd_r.at[h, i], x_dev(i))

    def c_ga(h, i):
        ref = gh.at[y, x, h, :, 0:hf]
        return copy(ref, ref, ga_s.at[h, i], ga_r.at[h, i], x_dev(i))

    def c_gb(h, i):
        ref = gh.at[y, x, h, :, hf:feats]
        return copy(ref, ref, gb_s.at[h, i], gb_r.at[h, i], y_dev(i))

    def c_gc(h, i):
        ref = gh.at[y, :, h, :, 0:hf]
        return copy(ref, ref, gc_s.at[h, i], gc_r.at[h, i], y_dev(i))

    def c_gd(h, i):
        ref = gh.at[:, x, h, :, hf:feats]
        return copy(ref, ref, gd_s.at[h, i], gd_r.at[h, i], x_dev(i))

    def logits_part(h, g):
        for n in range(gw // PIECE):
            cols = slice(n * PIECE, (n + 1) * PIECE)
            wide = slice(g * gw + n * PIECE, g * gw + (n + 1) * PIECE)
            part[h, g, :, cols] = jnp.dot(ag[h].reshape(HALF, feats), w[:, wide], preferred_element_type=F32)
            send(c_core, h, g, n)

    def reduce_core(h, g):
        for n in range(gw // PIECE):
            arrive(c_core, h, g, n)
        for ab in range(2):
            for s in range(2):
                at = send1[ab] + s * 16
                v = part[h, g, pl.ds(al(at), 16)] + core[h, g, pl.ds(al(at - k * 128), 16)]
                m1s[h, g, ab, s * 16:s * 16 + 16, 0:gw], m1s[h, g, ab, s * 16:s * 16 + 16, gw:] = coded(v)
            send(c_z1, h, g, ab)
        for ab in range(2):
            for s in range(2):
                at = keep1[ab] + s * 16
                part[h, g, pl.ds(al(at), 16)] += core[h, g, pl.ds(al(at - k * 128), 16)]

    def reduce_first(h, g):
        for ab in range(2):
            arrive(c_z1, h, g, ab)
            there = pl.ds(al((1 - second_side[ab]) * 16), 16)
            v = part[h, g, pl.ds(al(send2[ab]), 16)] + decoded(m1r[h, g, ab, there, 0:gw], m1r[h, g, ab, there, gw:])
            m2s[h, g, ab, :, 0:gw], m2s[h, g, ab, :, gw:] = coded(v)
            send(c_z2, h, g, ab)
        for ab in range(2):
            here = pl.ds(al(second_side[ab] * 16), 16)
            part[h, g, pl.ds(al(own[ab]), 16)] += decoded(m1r[h, g, ab, here, 0:gw], m1r[h, g, ab, here, gw:])

    def reduce_second(h, g):
        for ab in range(2):
            arrive(c_z2, h, g, ab)
            logit[h, ab * 16:ab * 16 + 16, g * gw:(g + 1) * gw] = part[h, g, pl.ds(al(own[ab]), 16)] + decoded(
                m2r[h, g, ab, :, 0:gw], m2r[h, g, ab, :, gw:]
            )

    vocab_start = col * width
    lane = lax.broadcasted_iota(I32, (16, 128), 1)
    cb = min(1024, width)

    def softmax_part(h):
        for ab in range(2):
            rows = slice(ab * 16, ab * 16 + 16)
            q = own[ab] // 16
            inv_col = inv[q, h * 16:h * 16 + 16, 0:1]
            t_col = tgt[h, pl.ds(al(own[ab]), 16), 0:1] - vocab_start
            top = jnp.full((16, 1), -jnp.inf, F32)
            for n in range(width // cb):
                cols = slice(n * cb, (n + 1) * cb)
                x = logit[h, rows, cols] * inv_col
                top = jnp.maximum(top, jnp.max(x, axis=1, keepdims=True))
            total = jnp.zeros((16, 1), F32)
            moment = jnp.zeros((16, 1), F32)
            target = jnp.zeros((16, 1), F32)
            for n in range(width // cb):
                cols = slice(n * cb, (n + 1) * cb)
                x = logit[h, rows, cols] * inv_col
                y = jnp.exp(x - top)
                e[h, pl.ds(al(own[ab]), 16), cols] = y.astype(BF)
                total += jnp.sum(y, axis=1, keepdims=True)
                moment += jnp.sum(y * x, axis=1, keepdims=True)
                ids = lax.broadcasted_iota(I32, (16, cb), 1) + n * cb
                target += jnp.sum(jnp.where(ids == t_col, x, 0.0), axis=1, keepdims=True)
            send(c_e1, h, ab)
            st[h, col, rows, :] = jnp.where(
                lane == 0, top, jnp.where(lane == 1, total, jnp.where(lane == 2, moment, target))
            )
        send(c_st, h, peers=COLS)

    def spread_first(h):
        for ab in range(2):
            arrive(c_e1, h, ab)
            send(c_e2, h, ab)
        for ab in range(2):
            send(c_e3, h, ab, 0)

    def spread_second(h):
        for ab in range(2):
            arrive(c_e2, h, ab)
            send(c_e3, h, ab, 1)

    def combine(h):
        arrive(c_st, h, peers=COLS)
        top = st[h, 0, :, 0:1]
        for j in range(1, COLS):
            top = jnp.maximum(top, st[h, j, :, 0:1])
        total, moment, target = (jnp.zeros((32, 1), F32) for _ in range(3))
        for j in range(COLS):
            s = st[h, j]
            scale = jnp.exp(s[:, 0:1] - top)
            total += s[:, 1:2] * scale
            moment += s[:, 2:3] * scale
            target += s[:, 3:4]
        mine = jnp.exp(st[h, col, :, 0:1] - top) / total
        curv = moment / total - target
        for ab in range(2):
            rows = slice(ab * 16, ab * 16 + 16)
            inv_col = inv[own[ab] // 16, h * 16:h * 16 + 16, 0:1]
            fac[h, row, rows, :] = jnp.where(lane == 0, mine[rows] * inv_col, curv[rows])
        send(c_fa, h, peers=ROWS)

    def prepare(h, whose):
        for ab in range(2):
            for late in range(2):
                if whose:
                    arrive(c_e3, h, ab, late)
        if not whose:
            arrive(c_fa, h, peers=ROWS)

        def group(t, carry):
            q = (k + whose - 2 * k * whose) * 8 + t
            r, ab = owner_row(q)
            f_col = fac[h, r, pl.ds(al(ab * 16), 16), 0:1]
            inv_col = inv[q, h * 16:h * 16 + 16, 0:1]
            rows = pl.ds(al(q * 16), 16)
            t_col = tgt[h, rows, 0:1] - vocab_start
            for n in range(width // cb):
                cols = slice(n * cb, (n + 1) * cb)
                ids = lax.broadcasted_iota(I32, (16, cb), 1) + n * cb
                v = e[h, rows, cols].astype(F32) * f_col - jnp.where(ids == t_col, inv_col, 0.0)
                grad[h, rows, cols] = v.astype(BF)
            return carry

        lax.fori_loop(0, 8, group, 0)

    def product(h):
        for n in range(QUARTERS):
            block = grad.at[h, :, n * width // QUARTERS:(n + 1) * width // QUARTERS]
            store(block, (grad_a, grad_b, grad_c, grad_d)[n].at[h], out_sem.at[3 + QUARTERS * h + n])

        for n in range(feats // 256):
            rows = slice(n * 256, (n + 1) * 256)
            v = lax.dot_general(grad[h], w[rows, :], NT, preferred_element_type=F32)
            fg[h, :, :, :, rows] = v.astype(BF).reshape(SIDE, SIDE, SUB, 256)
            if n == feats // 512 - 1:
                send(c_ra, h, peers=SIDE)
        send(c_rb, h, peers=SIDE)

    def sum_first(h):
        arrive(c_ra, h, peers=SIDE)
        total = fg[h, :, x, :, 0:hf].astype(F32)
        for i in range(1, SIDE):
            total = total + ra[h, i].astype(F32)
        ra[h, 0] = total.astype(BF)
        send(c_rc, h, peers=SIDE)
        arrive(c_rb, h, peers=SIDE)
        total = fg[h, y, :, :, hf:feats].astype(F32)
        for i in range(1, SIDE):
            total = total + rb[h, i].astype(F32)
        rb[h, 0] = total.astype(BF)
        send(c_rd, h, peers=SIDE)

    def residual(h):
        r, ab = owner_row(col)
        curv = fac[h, r, pl.ds(al(ab * 16), 16), 1:2]
        inv_col = inv[col, h * 16:h * 16 + 16, 0:1]
        factor = inv_col * inv_col * curv
        for half in range(2):
            cols = slice(half * hf, (half + 1) * hf)
            arrive((c_rc, c_rd)[half], h, peers=SIDE)
            total = (rb[h, 0, x] if half else ra[h, 0, y]).astype(F32)
            for i in range(1, SIDE):
                total = total + (rc, rd)[half][h, i].astype(F32)
            wide = hid[h * 16:h * 16 + 16, cols].astype(F32)
            v = (gain[:, cols] * total - wide * factor / D).astype(BF)
            gh[y, x, h, :, cols] = v
            send((c_ga, c_gb)[half], h, peers=SIDE)

    def pass_on(h):
        arrive(c_ga, h, peers=SIDE)
        send(c_gc, h, peers=SIDE)
        arrive(c_gb, h, peers=SIDE)
        send(c_gd, h, peers=SIDE)

    def enter():
        for n in range(3, 6):
            store(*loads[n])
        for n in range(3):
            store(*loads[n])
        barrier = pltpu.get_barrier_semaphore()
        each(COLS, lambda i: pl.semaphore_signal(barrier, inc=1, device_id=col_dev(i), device_id_type=MESH))
        each(ROWS, lambda i: pl.semaphore_signal(barrier, inc=1, device_id=row_dev(i), device_id_type=MESH))
        for n in range(3, 6):
            stored(n)
        for h in range(2):
            v = hid[h * 16:h * 16 + 16, :].astype(F32)
            ag[h, y, x] = (gain[...] * v).astype(BF)
            sq[row, h * 16:h * 16 + 16, :] = jnp.broadcast_to(jnp.sum(v * v, axis=1, keepdims=True), (16, 128))
        pl.semaphore_wait(barrier, COLS + ROWS - 2)
        send(c_aa, 0, peers=SIDE)
        send(c_ab, 0, peers=SIDE)
        send(c_sq, peers=ROWS)

    def order_targets():
        ids = jnp.concatenate([tgt_in[...], tgt_in[...]], axis=0).astype(F32).T
        for j in range(COLS):
            for h in range(2):
                at = (j % 4) * 32 + h * 16
                ids_col = ids[at:at + 16, j // 4:j // 4 + 1].astype(I32)
                tgt[h, j * 16:j * 16 + 16, :] = jnp.broadcast_to(ids_col, (16, 128))

    def squares():
        arrive(c_sq, peers=ROWS)
        total = sq[0]
        for r in range(1, ROWS):
            total = total + sq[r]
        inv[col] = 1.0 / jnp.sqrt(total / D + EPS)
        send(c_inv, peers=COLS)

    def activate():
        stored(1)
        stored(2)

        @pl.loop(0, gate.shape[1] // 128)
        def _(n):
            cols = pl.ds(al(n * 128, 128), 128)
            v = gate[:, cols].astype(F32)
            act[cols, :] = (v / (1.0 + jnp.exp(-v)) * up[:, cols].astype(F32)).T.astype(BF)

        store(act, act_out, out_sem.at[1])

    def turn(h):
        at = slice(h * HALF, (h + 1) * HALF)
        for n in range(feats // 256):
            rows = slice(n * 256, (n + 1) * 256)
            turned[rows, at] = ag[h, :, :, :, rows].reshape(HALF, 256).T
        if h == 1:
            store(turned, scaled_out, out_sem.at[2])

    def gather_on(h):
        arrive(c_aa, h, peers=SIDE)
        send(c_ac, h, peers=SIDE)
        arrive(c_ab, h, peers=SIDE)
        send(c_ad, h, peers=SIDE)
        if h == 0:
            send(c_aa, 1, peers=SIDE)
            send(c_ab, 1, peers=SIDE)

    def gathered(h):
        arrive(c_ac, h, peers=SIDE)
        arrive(c_ad, h, peers=SIDE)

    def scales():
        arrive(c_inv, peers=COLS)

    def finish():
        for h in range(2):
            arrive(c_gc, h, peers=SIDE)
            arrive(c_gd, h, peers=SIDE)
        store(gh, all_out, out_sem.at[0])

    steps = [
        (enter,), (gather_on, 0), (order_targets,), (activate,), (stored, 0),
        (gathered, 0), (logits_part, 0, 0), (gather_on, 1), (logits_part, 0, 1), (reduce_core, 0, 0),
        (reduce_core, 0, 1), (squares,), (gathered, 1), (logits_part, 1, 0), (reduce_first, 0, 0), (logits_part, 1, 1),
        (reduce_first, 0, 1), (reduce_core, 1, 0), (reduce_core, 1, 1), (turn, 0), (turn, 1),
        (scales,), (reduce_second, 0, 0), (reduce_second, 0, 1), (softmax_part, 0),
        (reduce_first, 1, 0), (reduce_first, 1, 1), (spread_first, 0),
        (reduce_second, 1, 0), (reduce_second, 1, 1), (softmax_part, 1),
        (combine, 0), (spread_second, 0), (spread_first, 1), (prepare, 0, 0), (prepare, 0, 1), (combine, 1),
        (product, 0), (spread_second, 1), (prepare, 1, 0), (prepare, 1, 1), (product, 1),
        (sum_first, 0), (residual, 0), (sum_first, 1), (pass_on, 0), (residual, 1), (pass_on, 1), (finish,),
    ]
    for step, *which in steps[:STOP]:
        step(*which)
    for make, key, peers in list(coming):
        arrive(make, *key, peers=peers)
    for make, key, peers in started:
        left(make, key, peers)
    for src, dst, sem in stores:
        pltpu.make_async_copy(src, dst, sem).wait()


def weights_kernel(scaled, grad_a, grad_b, grad_c, grad_d, act, resid, head, down, own):
    i = pl.program_id(0)
    for n, grad in enumerate((grad_a, grad_b, grad_c, grad_d)):

        @pl.when(i == n)
        def _(grad=grad):
            block = grad[...].reshape(2 * HALF, head.shape[1])
            head[...] = jnp.dot(scaled[...], block, preferred_element_type=F32).astype(BF)

    down[...] = jnp.dot(act[...], resid[...], preferred_element_type=F32).astype(BF)

    @pl.when(i == 0)
    def _():
        own[...] = resid[pl.ds(pl.multiple_of(lax.axis_index("col") * 32, 32), 32), :]


def on_device(hidden_state, norm_gain, head_weight, targets, gate_act, up_act):
    feats, width = head_weight.shape
    gw = width // G
    tokens = 2 * HALF
    hidden_units = gate_act.shape[1]
    vm, hbm = pl.BlockSpec(memory_space=pltpu.VMEM), pl.BlockSpec(memory_space=pl.ANY)
    dma = pltpu.SemaphoreType.DMA

    def pair(*shape):
        return [dma(shape), dma(shape)]

    *grads, scaled, resid, act = pl.pallas_call(
        kernel,
        out_shape=(
            *[jax.ShapeDtypeStruct((2, HALF, width // QUARTERS), BF)] * QUARTERS,
            jax.ShapeDtypeStruct((feats, tokens), BF),
            jax.ShapeDtypeStruct((SIDE, SIDE, 2, SUB, feats), BF),
            jax.ShapeDtypeStruct((hidden_units, tokens), BF),
        ),
        in_specs=[pl.BlockSpec(memory_space=pltpu.HBM)] * 6,
        out_specs=(*[hbm] * 7,),
        scratch_shapes=[
            pltpu.VMEM(hidden_state.shape, BF),
            pltpu.VMEM((1, feats), F32),
            pltpu.VMEM((4, 128), I32),
            pltpu.VMEM((feats, width), BF),
            pltpu.VMEM((tokens, hidden_units), BF),
            pltpu.VMEM((tokens, hidden_units), BF),
            pltpu.VMEM((hidden_units, tokens), BF),
            pltpu.VMEM((feats, tokens), BF),
            pltpu.VMEM((2, HALF, 128), I32),
            pltpu.VMEM((2, SIDE, SIDE, SUB, feats), BF),
            pltpu.VMEM((ROWS, 32, 128), F32),
            pltpu.VMEM((COLS, 32, 128), F32),
            pltpu.VMEM((2, G, HALF, gw), F32),
            pltpu.VMEM((2, G, HALF // 2, gw), F32),
            pltpu.VMEM((2, G, 2, 32, gw + TAIL), I16),
            pltpu.VMEM((2, G, 2, 32, gw + TAIL), I16),
            pltpu.VMEM((2, G, 2, 16, gw + TAIL), I16),
            pltpu.VMEM((2, G, 2, 16, gw + TAIL), I16),
            pltpu.VMEM((2, 32, width), F32),
            pltpu.VMEM((2, HALF, width), BF),
            pltpu.VMEM((2, HALF, width), BF),
            pltpu.VMEM((2, COLS, 32, 128), F32),
            pltpu.VMEM((2, ROWS, 32, 128), F32),
            pltpu.VMEM((2, SIDE, SIDE, SUB, feats), BF),
            pltpu.VMEM((2, SIDE, SIDE, SUB, feats // 2), BF),
            pltpu.VMEM((2, SIDE, SIDE, SUB, feats // 2), BF),
            pltpu.VMEM((2, SIDE, SUB, feats // 2), BF),
            pltpu.VMEM((2, SIDE, SUB, feats // 2), BF),
            pltpu.VMEM((SIDE, SIDE, 2, SUB, feats), BF),
            dma((6,)), dma((11,)),
            *pair(ROWS), *pair(COLS), *pair(2, G, gw // PIECE), *pair(2, G, 2), *pair(2, G, 2),
            *pair(2, 2), *pair(2, 2), *pair(2, 2, 2), *pair(2, COLS), *pair(2, ROWS),
            *[dma((2, SIDE))] * 24,
        ],
        compiler_params=pltpu.CompilerParams(
            collective_id=0, has_side_effects=True, vmem_limit_bytes=46 * 2**20
        ),
        name="head_backward",
    )(hidden_state, norm_gain.reshape(1, feats), targets.reshape(4, 128), head_weight, gate_act, up_act)
    tiles = QUARTERS
    head_grad, down_grad, grad_hidden = pl.pallas_call(
        weights_kernel,
        grid=(tiles,),
        out_shape=(
            jax.ShapeDtypeStruct((feats, width), BF),
            jax.ShapeDtypeStruct((hidden_units, feats), BF),
            jax.ShapeDtypeStruct(hidden_state.shape, BF),
        ),
        in_specs=[vm] * 5 + [pl.BlockSpec((hidden_units // tiles, tokens), lambda i: (i, 0)), vm],
        out_specs=(
            pl.BlockSpec((feats, width // tiles), lambda i: (0, i)),
            pl.BlockSpec((hidden_units // tiles, feats), lambda i: (i, 0)),
            pl.BlockSpec(hidden_state.shape, lambda i: (0, 0)),
        ),
        compiler_params=pltpu.CompilerParams(vmem_limit_bytes=24 * 2**20),
        name="weight_gradients",
    )(scaled, *grads, act, resid.reshape(tokens, feats))
    return head_grad, grad_hidden, down_grad


def solution(mesh):
    in_specs = (P("col", "row"), P("row"), P("row", "col"), P(), P(None, "col"), P(None, "col"))
    out_specs = (P("row", "col"), P("col", "row"), P("col", "row"))
    return jax.shard_map(
        on_device, mesh=mesh, in_specs=in_specs, out_specs=out_specs, check_vma=False
    )
```

```python
import jax
import jax.numpy as jnp
from jax import lax
from jax.experimental import pallas as pl
from jax.experimental.pallas import tpu as pltpu
from jax.sharding import PartitionSpec as P

D = 8192
EPS = 1e-05
BF, F32, I16, I32 = jnp.bfloat16, jnp.float32, jnp.int16, jnp.int32
MESH = pl.DeviceIdType.MESH
COLS, ROWS = 16, 8
SIDE = 4
PIECE = 512
QUARTERS = 4
G = 2
SUB = 16
HALF = SUB * COLS
TAIL = 128
CODES = 32000.0
FINE = 64.0
STOP = None
NT = (((1,), (1,)), ((), ()))


def coded(values):
    most = jnp.maximum(jnp.max(jnp.abs(values), axis=1, keepdims=True), 1e-30)
    level = jnp.ceil(jnp.log2(most) * FINE)
    codes = jnp.round(values * (jnp.exp2(level * (-1.0 / FINE)) * CODES))
    return codes.astype(I32).astype(I16), jnp.broadcast_to(level, (values.shape[0], TAIL)).astype(I32).astype(I16)


def decoded(codes, tail):
    level = tail.astype(I32).astype(F32)[:, 0:1]
    return codes.astype(I32).astype(F32) * (jnp.exp2(level * (1.0 / FINE)) * (1.0 / CODES))


def owner_row(q):
    k, ab, b1, b0 = q // 8, (q // 4) % 2, (q // 2) % 2, q % 2
    s_a = jnp.where(ab == 0, b1, b0)
    s_b = jnp.where(ab == 0, b0, b1)
    return (s_b * 2 + (s_a + s_b) % 2) * 2 + k, ab


def kernel(
    hid_hbm, gain_hbm, tgt_hbm, w_hbm, gate_hbm, up_hbm,
    grad_a, grad_b, grad_c, grad_d, scaled_out, all_out, act_out,
    hid, gain, tgt_in, w, gate, up, act, turned, tgt, ag, sq, inv, part, core, m1s, m1r, m2s, m2r, logit, e, grad, st, fac, fg, ra, rb, rc, rd, gh,
    in_sem, out_sem, sq_s, sq_r, inv_s, inv_r, c_s, c_r, z1_s, z1_r, z2_s, z2_r,
    e1_s, e1_r, e2_s, e2_r, e3_s, e3_r, st_s, st_r, fa_s, fa_r,
    aa_s, aa_r, ab_s, ab_r, ac_s, ac_r, ad_s, ad_r, ra_s, ra_r, rb_s, rb_r, rc_s, rc_r, rd_s, rd_r,
    ga_s, ga_r, gb_s, gb_r, gc_s, gc_r, gd_s, gd_r,
):
    row, col = lax.axis_index("row"), lax.axis_index("col")
    z, k = row // 2, row % 2
    hi = z // 2
    s_a = (hi + z) % 2
    s_b = hi
    width = w.shape[1]
    feats = w.shape[0]
    gw = width // G
    hf = feats // 2
    dev_core = (z * 2 + (1 - k), col)
    dev_a = ((z + 1 - 2 * (z % 2)) * 2 + k, col)
    dev_b = (((z + 3 + 2 * (z % 2)) % 4) * 2 + k, col)
    first_side = (s_a, s_b)
    second_side = (s_b, s_a)
    first_dev = (dev_a, dev_b)
    second_dev = (dev_b, dev_a)
    keep1 = [k * 128 + ab * 64 + first_side[ab] * 32 for ab in range(2)]
    send1 = [k * 128 + ab * 64 + (1 - first_side[ab]) * 32 for ab in range(2)]
    own = [keep1[ab] + second_side[ab] * 16 for ab in range(2)]
    send2 = [keep1[ab] + (1 - second_side[ab]) * 16 for ab in range(2)]

    def al(v, n=16):
        return pl.multiple_of(v, n)

    started, coming, stores = [], [], []
    loads = [(w_hbm, w, in_sem.at[0]), (gate_hbm, gate, in_sem.at[1]), (up_hbm, up, in_sem.at[2])]
    loads += [(hid_hbm, hid, in_sem.at[3]), (gain_hbm, gain, in_sem.at[4]), (tgt_hbm, tgt_in, in_sem.at[5])]

    def copy(src, dst, ss, rs, dev):
        return pltpu.make_async_remote_copy(
            src_ref=src, dst_ref=dst, send_sem=ss, recv_sem=rs, device_id=dev, device_id_type=MESH
        )

    def send(make, *key, peers=None):
        started.append((make, key, peers))
        coming.append((make, key, peers))
        if peers:
            each(peers, lambda i: make(*key, i).start())
        else:
            make(*key).start()

    def arrive(make, *key, peers=None):
        coming.remove((make, key, peers))
        if peers:
            each(peers, lambda i: make(*key, i).wait_recv())
        else:
            make(*key).wait_recv()

    def store(src, dst, sem):
        stores.append((src, dst, sem))
        pltpu.make_async_copy(src, dst, sem).start()

    def stored(n):
        src, dst, sem = loads[n]
        del stores[[d is dst for _, d, _ in stores].index(True)]
        pltpu.make_async_copy(src, dst, sem).wait()

    def left(make, key, peers):
        if peers:
            each(peers, lambda i: make(*key, i).wait_send())
        else:
            make(*key).wait_send()

    def col_dev(i):
        return (row, lax.rem(col + i, COLS))

    x, y = col % SIDE, col // SIDE

    def x_dev(i):
        return (row, y * SIDE + lax.rem(x + i, SIDE))

    def y_dev(i):
        return (row, lax.rem(y + i, SIDE) * SIDE + x)

    def row_dev(i):
        return (lax.rem(row + i, ROWS), col)

    def each(n, fn):
        def body(i, carry):
            fn(i)
            return carry

        lax.fori_loop(1, n, body, 0)

    def c_aa(h, i):
        ref = ag.at[h, y, x, :, 0:hf]
        return copy(ref, ref, aa_s.at[h, i], aa_r.at[h, i], x_dev(i))

    def c_ab(h, i):
        ref = ag.at[h, y, x, :, hf:feats]
        return copy(ref, ref, ab_s.at[h, i], ab_r.at[h, i], y_dev(i))

    def c_ac(h, i):
        ref = ag.at[h, y, :, :, 0:hf]
        return copy(ref, ref, ac_s.at[h, i], ac_r.at[h, i], y_dev(i))

    def c_ad(h, i):
        ref = ag.at[h, :, x, :, hf:feats]
        return copy(ref, ref, ad_s.at[h, i], ad_r.at[h, i], x_dev(i))

    def c_sq(i):
        return copy(sq.at[row], sq.at[row], sq_s.at[i], sq_r.at[i], row_dev(i))

    def c_inv(i):
        return copy(inv.at[col], inv.at[col], inv_s.at[i], inv_r.at[i], col_dev(i))

    def c_core(h, g, n):
        cols = pl.ds(al(n * PIECE, PIECE), PIECE)
        return copy(
            part.at[h, g, pl.ds(al((1 - k) * 128), 128), cols], core.at[h, g, :, cols],
            c_s.at[h, g, n], c_r.at[h, g, n], dev_core,
        )

    def c_z1(h, g, ab):
        return copy(m1s.at[h, g, ab], m1r.at[h, g, ab], z1_s.at[h, g, ab], z1_r.at[h, g, ab], first_dev[ab])

    def c_z2(h, g, ab):
        return copy(m2s.at[h, g, ab], m2r.at[h, g, ab], z2_s.at[h, g, ab], z2_r.at[h, g, ab], second_dev[ab])

    def c_e1(h, ab):
        ref = e.at[h, pl.ds(al(own[ab]), 16)]
        return copy(ref, ref, e1_s.at[h, ab], e1_r.at[h, ab], second_dev[ab])

    def c_e2(h, ab):
        ref = e.at[h, pl.ds(al(keep1[ab]), 32)]
        return copy(ref, ref, e2_s.at[h, ab], e2_r.at[h, ab], first_dev[ab])

    def c_e3(h, ab, late):
        ref = e.at[h, pl.ds(al((send1 if late else keep1)[ab]), 32)]
        return copy(ref, ref, e3_s.at[h, ab, late], e3_r.at[h, ab, late], dev_core)

    def c_st(h, i):
        return copy(st.at[h, col], st.at[h, col], st_s.at[h, i], st_r.at[h, i], col_dev(i))

    def c_fa(h, i):
        return copy(fac.at[h, row], fac.at[h, row], fa_s.at[h, i], fa_r.at[h, i], row_dev(i))

    def c_ra(h, i):
        return copy(fg.at[h, :, lax.rem(x + i, SIDE), :, 0:hf], ra.at[h, i], ra_s.at[h, i], ra_r.at[h, i], x_dev(i))

    def c_rb(h, i):
        return copy(fg.at[h, lax.rem(y + i, SIDE), :, :, hf:feats], rb.at[h, i], rb_s.at[h, i], rb_r.at[h, i], y_dev(i))

    def c_rc(h, i):
        return copy(ra.at[h, 0, lax.rem(y + i, SIDE)], rc.at[h, i], rc_s.at[h, i], rc_r.at[h, i], y_dev(i))

    def c_rd(h, i):
        return copy(rb.at[h, 0, lax.rem(x + i, SIDE)], rd.at[h, i], rd_s.at[h, i], rd_r.at[h, i], x_dev(i))

    def c_ga(h, i):
        ref = gh.at[y, x, h, :, 0:hf]
        return copy(ref, ref, ga_s.at[h, i], ga_r.at[h, i], x_dev(i))

    def c_gb(h, i):
        ref = gh.at[y, x, h, :, hf:feats]
        return copy(ref, ref, gb_s.at[h, i], gb_r.at[h, i], y_dev(i))

    def c_gc(h, i):
        ref = gh.at[y, :, h, :, 0:hf]
        return copy(ref, ref, gc_s.at[h, i], gc_r.at[h, i], y_dev(i))

    def c_gd(h, i):
        ref = gh.at[:, x, h, :, hf:feats]
        return copy(ref, ref, gd_s.at[h, i], gd_r.at[h, i], x_dev(i))

    def logits_part(h, g):
        for n in range(gw // PIECE):
            cols = slice(n * PIECE, (n + 1) * PIECE)
            wide = slice(g * gw + n * PIECE, g * gw + (n + 1) * PIECE)
            part[h, g, :, cols] = jnp.dot(ag[h].reshape(HALF, feats), w[:, wide], preferred_element_type=F32)
            send(c_core, h, g, n)

    def reduce_core(h, g):
        for n in range(gw // PIECE):
            arrive(c_core, h, g, n)
        for ab in range(2):
            for s in range(2):
                at = send1[ab] + s * 16
                v = part[h, g, pl.ds(al(at), 16)] + core[h, g, pl.ds(al(at - k * 128), 16)]
                m1s[h, g, ab, s * 16:s * 16 + 16, 0:gw], m1s[h, g, ab, s * 16:s * 16 + 16, gw:] = coded(v)
            send(c_z1, h, g, ab)
        for ab in range(2):
            for s in range(2):
                at = keep1[ab] + s * 16
                part[h, g, pl.ds(al(at), 16)] += core[h, g, pl.ds(al(at - k * 128), 16)]

    def reduce_first(h, g):
        for ab in range(2):
            arrive(c_z1, h, g, ab)
            there = pl.ds(al((1 - second_side[ab]) * 16), 16)
            v = part[h, g, pl.ds(al(send2[ab]), 16)] + decoded(m1r[h, g, ab, there, 0:gw], m1r[h, g, ab, there, gw:])
            m2s[h, g, ab, :, 0:gw], m2s[h, g, ab, :, gw:] = coded(v)
            send(c_z2, h, g, ab)
        for ab in range(2):
            here = pl.ds(al(second_side[ab] * 16), 16)
            part[h, g, pl.ds(al(own[ab]), 16)] += decoded(m1r[h, g, ab, here, 0:gw], m1r[h, g, ab, here, gw:])

    def reduce_second(h, g):
        for ab in range(2):
            arrive(c_z2, h, g, ab)
            logit[h, ab * 16:ab * 16 + 16, g * gw:(g + 1) * gw] = part[h, g, pl.ds(al(own[ab]), 16)] + decoded(
                m2r[h, g, ab, :, 0:gw], m2r[h, g, ab, :, gw:]
            )

    vocab_start = col * width
    lane = lax.broadcasted_iota(I32, (16, 128), 1)
    cb = min(1024, width)

    def softmax_part(h):
        for ab in range(2):
            rows = slice(ab * 16, ab * 16 + 16)
            q = own[ab] // 16
            inv_col = inv[q, h * 16:h * 16 + 16, 0:1]
            t_col = tgt[h, pl.ds(al(own[ab]), 16), 0:1] - vocab_start
            top = jnp.full((16, 1), -jnp.inf, F32)
            for n in range(width // cb):
                cols = slice(n * cb, (n + 1) * cb)
                x = logit[h, rows, cols] * inv_col
                top = jnp.maximum(top, jnp.max(x, axis=1, keepdims=True))
            total = jnp.zeros((16, 1), F32)
            moment = jnp.zeros((16, 1), F32)
            target = jnp.zeros((16, 1), F32)
            for n in range(width // cb):
                cols = slice(n * cb, (n + 1) * cb)
                x = logit[h, rows, cols] * inv_col
                y = jnp.exp(x - top)
                e[h, pl.ds(al(own[ab]), 16), cols] = y.astype(BF)
                total += jnp.sum(y, axis=1, keepdims=True)
                moment += jnp.sum(y * x, axis=1, keepdims=True)
                ids = lax.broadcasted_iota(I32, (16, cb), 1) + n * cb
                target += jnp.sum(jnp.where(ids == t_col, x, 0.0), axis=1, keepdims=True)
            send(c_e1, h, ab)
            st[h, col, rows, :] = jnp.where(
                lane == 0, top, jnp.where(lane == 1, total, jnp.where(lane == 2, moment, target))
            )
        send(c_st, h, peers=COLS)

    def spread_first(h):
        for ab in range(2):
            arrive(c_e1, h, ab)
            send(c_e2, h, ab)
        for ab in range(2):
            send(c_e3, h, ab, 0)

    def spread_second(h):
        for ab in range(2):
            arrive(c_e2, h, ab)
            send(c_e3, h, ab, 1)

    def combine(h):
        arrive(c_st, h, peers=COLS)
        top = st[h, 0, :, 0:1]
        for j in range(1, COLS):
            top = jnp.maximum(top, st[h, j, :, 0:1])
        total, moment, target = (jnp.zeros((32, 1), F32) for _ in range(3))
        for j in range(COLS):
            s = st[h, j]
            scale = jnp.exp(s[:, 0:1] - top)
            total += s[:, 1:2] * scale
            moment += s[:, 2:3] * scale
            target += s[:, 3:4]
        mine = jnp.exp(st[h, col, :, 0:1] - top) / total
        curv = moment / total - target
        for ab in range(2):
            rows = slice(ab * 16, ab * 16 + 16)
            inv_col = inv[own[ab] // 16, h * 16:h * 16 + 16, 0:1]
            fac[h, row, rows, :] = jnp.where(lane == 0, mine[rows] * inv_col, curv[rows])
        send(c_fa, h, peers=ROWS)

    def prepare(h, whose):
        for ab in range(2):
            for late in range(2):
                if whose:
                    arrive(c_e3, h, ab, late)
        if not whose:
            arrive(c_fa, h, peers=ROWS)

        def group(t, carry):
            q = (k + whose - 2 * k * whose) * 8 + t
            r, ab = owner_row(q)
            f_col = fac[h, r, pl.ds(al(ab * 16), 16), 0:1]
            inv_col = inv[q, h * 16:h * 16 + 16, 0:1]
            rows = pl.ds(al(q * 16), 16)
            t_col = tgt[h, rows, 0:1] - vocab_start
            for n in range(width // cb):
                cols = slice(n * cb, (n + 1) * cb)
                ids = lax.broadcasted_iota(I32, (16, cb), 1) + n * cb
                v = e[h, rows, cols].astype(F32) * f_col - jnp.where(ids == t_col, inv_col, 0.0)
                grad[h, rows, cols] = v.astype(BF)
            return carry

        lax.fori_loop(0, 8, group, 0)

    def product(h, half):
        if half == 0:
            for n in range(QUARTERS):
                block = grad.at[h, :, n * width // QUARTERS:(n + 1) * width // QUARTERS]
                store(block, (grad_a, grad_b, grad_c, grad_d)[n].at[h], out_sem.at[3 + QUARTERS * h + n])
        for n in range(half * hf // 256, (half + 1) * hf // 256):
            rows = slice(n * 256, (n + 1) * 256)
            v = lax.dot_general(grad[h], w[rows, :], NT, preferred_element_type=F32)
            fg[h, :, :, :, rows] = v.astype(BF).reshape(SIDE, SIDE, SUB, 256)
        send((c_ra, c_rb)[half], h, peers=SIDE)

    def sum_first(h):
        arrive(c_ra, h, peers=SIDE)
        total = fg[h, :, x, :, 0:hf].astype(F32)
        for i in range(1, SIDE):
            total = total + ra[h, i].astype(F32)
        ra[h, 0] = total.astype(BF)
        send(c_rc, h, peers=SIDE)
        arrive(c_rb, h, peers=SIDE)
        total = fg[h, y, :, :, hf:feats].astype(F32)
        for i in range(1, SIDE):
            total = total + rb[h, i].astype(F32)
        rb[h, 0] = total.astype(BF)
        send(c_rd, h, peers=SIDE)

    def residual(h):
        r, ab = owner_row(col)
        curv = fac[h, r, pl.ds(al(ab * 16), 16), 1:2]
        inv_col = inv[col, h * 16:h * 16 + 16, 0:1]
        factor = inv_col * inv_col * curv
        for half in range(2):
            cols = slice(half * hf, (half + 1) * hf)
            arrive((c_rc, c_rd)[half], h, peers=SIDE)
            total = (rb[h, 0, x] if half else ra[h, 0, y]).astype(F32)
            for i in range(1, SIDE):
                total = total + (rc, rd)[half][h, i].astype(F32)
            wide = hid[h * 16:h * 16 + 16, cols].astype(F32)
            v = (gain[:, cols] * total - wide * factor / D).astype(BF)
            gh[y, x, h, :, cols] = v
            send((c_ga, c_gb)[half], h, peers=SIDE)

    def pass_on(h):
        arrive(c_ga, h, peers=SIDE)
        send(c_gc, h, peers=SIDE)
        arrive(c_gb, h, peers=SIDE)
        send(c_gd, h, peers=SIDE)

    def enter():
        for n in range(3, 6):
            store(*loads[n])
        for n in range(3):
            store(*loads[n])
        barrier = pltpu.get_barrier_semaphore()
        each(COLS, lambda i: pl.semaphore_signal(barrier, inc=1, device_id=col_dev(i), device_id_type=MESH))
        each(ROWS, lambda i: pl.semaphore_signal(barrier, inc=1, device_id=row_dev(i), device_id_type=MESH))
        for n in range(3, 6):
            stored(n)
        for h in range(2):
            v = hid[h * 16:h * 16 + 16, :].astype(F32)
            ag[h, y, x] = (gain[...] * v).astype(BF)
            sq[row, h * 16:h * 16 + 16, :] = jnp.broadcast_to(jnp.sum(v * v, axis=1, keepdims=True), (16, 128))
        pl.semaphore_wait(barrier, COLS + ROWS - 2)
        send(c_aa, 0, peers=SIDE)
        send(c_ab, 0, peers=SIDE)
        send(c_sq, peers=ROWS)

    def order_targets():
        ids = jnp.concatenate([tgt_in[...], tgt_in[...]], axis=0).astype(F32).T
        for j in range(COLS):
            for h in range(2):
                at = (j % 4) * 32 + h * 16
                ids_col = ids[at:at + 16, j // 4:j // 4 + 1].astype(I32)
                tgt[h, j * 16:j * 16 + 16, :] = jnp.broadcast_to(ids_col, (16, 128))

    def squares():
        arrive(c_sq, peers=ROWS)
        total = sq[0]
        for r in range(1, ROWS):
            total = total + sq[r]
        inv[col] = 1.0 / jnp.sqrt(total / D + EPS)
        send(c_inv, peers=COLS)

    def activate():
        stored(1)
        stored(2)

        @pl.loop(0, gate.shape[1] // 128)
        def _(n):
            cols = pl.ds(al(n * 128, 128), 128)
            v = gate[:, cols].astype(F32)
            act[cols, :] = (v / (1.0 + jnp.exp(-v)) * up[:, cols].astype(F32)).T.astype(BF)

        store(act, act_out, out_sem.at[1])

    def turn(h):
        at = slice(h * HALF, (h + 1) * HALF)
        for n in range(feats // 256):
            rows = slice(n * 256, (n + 1) * 256)
            turned[rows, at] = ag[h, :, :, :, rows].reshape(HALF, 256).T
        if h == 1:
            store(turned, scaled_out, out_sem.at[2])

    def gather_on(h):
        arrive(c_aa, h, peers=SIDE)
        send(c_ac, h, peers=SIDE)
        arrive(c_ab, h, peers=SIDE)
        send(c_ad, h, peers=SIDE)
        if h == 0:
            send(c_aa, 1, peers=SIDE)
            send(c_ab, 1, peers=SIDE)

    def gathered(h):
        arrive(c_ac, h, peers=SIDE)
        arrive(c_ad, h, peers=SIDE)

    def scales():
        arrive(c_inv, peers=COLS)

    def finish():
        for h in range(2):
            arrive(c_gc, h, peers=SIDE)
            arrive(c_gd, h, peers=SIDE)
        store(gh, all_out, out_sem.at[0])

    steps = [
        (enter,), (gather_on, 0), (order_targets,), (activate,), (stored, 0),
        (gathered, 0), (logits_part, 0, 0), (gather_on, 1), (logits_part, 0, 1), (reduce_core, 0, 0),
        (reduce_core, 0, 1), (squares,), (gathered, 1), (logits_part, 1, 0), (reduce_first, 0, 0), (logits_part, 1, 1),
        (reduce_first, 0, 1), (reduce_core, 1, 0), (reduce_core, 1, 1), (turn, 0), (turn, 1),
        (scales,), (reduce_second, 0, 0), (reduce_second, 0, 1), (softmax_part, 0),
        (reduce_first, 1, 0), (reduce_first, 1, 1), (spread_first, 0),
        (reduce_second, 1, 0), (reduce_second, 1, 1), (softmax_part, 1),
        (combine, 0), (spread_second, 0), (spread_first, 1), (prepare, 0, 0), (prepare, 0, 1), (combine, 1),
        (product, 0, 0), (spread_second, 1), (product, 0, 1), (prepare, 1, 0), (prepare, 1, 1), (product, 1, 0), (product, 1, 1),
        (sum_first, 0), (residual, 0), (sum_first, 1), (pass_on, 0), (residual, 1), (pass_on, 1), (finish,),
    ]
    for step, *which in steps[:STOP]:
        step(*which)
    for make, key, peers in list(coming):
        arrive(make, *key, peers=peers)
    for make, key, peers in started:
        left(make, key, peers)
    for src, dst, sem in stores:
        pltpu.make_async_copy(src, dst, sem).wait()


def weights_kernel(scaled, grad_a, grad_b, grad_c, grad_d, act, resid, head, down, own):
    i = pl.program_id(0)
    for n, grad in enumerate((grad_a, grad_b, grad_c, grad_d)):

        @pl.when(i == n)
        def _(grad=grad):
            block = grad[...].reshape(2 * HALF, head.shape[1])
            head[...] = jnp.dot(scaled[...], block, preferred_element_type=F32).astype(BF)

    down[...] = jnp.dot(act[...], resid[...], preferred_element_type=F32).astype(BF)

    @pl.when(i == 0)
    def _():
        own[...] = resid[pl.ds(pl.multiple_of(lax.axis_index("col") * 32, 32), 32), :]


def on_device(hidden_state, norm_gain, head_weight, targets, gate_act, up_act):
    feats, width = head_weight.shape
    gw = width // G
    tokens = 2 * HALF
    hidden_units = gate_act.shape[1]
    vm, hbm = pl.BlockSpec(memory_space=pltpu.VMEM), pl.BlockSpec(memory_space=pl.ANY)
    dma = pltpu.SemaphoreType.DMA

    def pair(*shape):
        return [dma(shape), dma(shape)]

    *grads, scaled, resid, act = pl.pallas_call(
        kernel,
        out_shape=(
            *[jax.ShapeDtypeStruct((2, HALF, width // QUARTERS), BF)] * QUARTERS,
            jax.ShapeDtypeStruct((feats, tokens), BF),
            jax.ShapeDtypeStruct((SIDE, SIDE, 2, SUB, feats), BF),
            jax.ShapeDtypeStruct((hidden_units, tokens), BF),
        ),
        in_specs=[pl.BlockSpec(memory_space=pltpu.HBM)] * 6,
        out_specs=(*[hbm] * 7,),
        scratch_shapes=[
            pltpu.VMEM(hidden_state.shape, BF),
            pltpu.VMEM((1, feats), F32),
            pltpu.VMEM((4, 128), I32),
            pltpu.VMEM((feats, width), BF),
            pltpu.VMEM((tokens, hidden_units), BF),
            pltpu.VMEM((tokens, hidden_units), BF),
            pltpu.VMEM((hidden_units, tokens), BF),
            pltpu.VMEM((feats, tokens), BF),
            pltpu.VMEM((2, HALF, 128), I32),
            pltpu.VMEM((2, SIDE, SIDE, SUB, feats), BF),
            pltpu.VMEM((ROWS, 32, 128), F32),
            pltpu.VMEM((COLS, 32, 128), F32),
            pltpu.VMEM((2, G, HALF, gw), F32),
            pltpu.VMEM((2, G, HALF // 2, gw), F32),
            pltpu.VMEM((2, G, 2, 32, gw + TAIL), I16),
            pltpu.VMEM((2, G, 2, 32, gw + TAIL), I16),
            pltpu.VMEM((2, G, 2, 16, gw + TAIL), I16),
            pltpu.VMEM((2, G, 2, 16, gw + TAIL), I16),
            pltpu.VMEM((2, 32, width), F32),
            pltpu.VMEM((2, HALF, width), BF),
            pltpu.VMEM((2, HALF, width), BF),
            pltpu.VMEM((2, COLS, 32, 128), F32),
            pltpu.VMEM((2, ROWS, 32, 128), F32),
            pltpu.VMEM((2, SIDE, SIDE, SUB, feats), BF),
            pltpu.VMEM((2, SIDE, SIDE, SUB, feats // 2), BF),
            pltpu.VMEM((2, SIDE, SIDE, SUB, feats // 2), BF),
            pltpu.VMEM((2, SIDE, SUB, feats // 2), BF),
            pltpu.VMEM((2, SIDE, SUB, feats // 2), BF),
            pltpu.VMEM((SIDE, SIDE, 2, SUB, feats), BF),
            dma((6,)), dma((11,)),
            *pair(ROWS), *pair(COLS), *pair(2, G, gw // PIECE), *pair(2, G, 2), *pair(2, G, 2),
            *pair(2, 2), *pair(2, 2), *pair(2, 2, 2), *pair(2, COLS), *pair(2, ROWS),
            *[dma((2, SIDE))] * 24,
        ],
        compiler_params=pltpu.CompilerParams(
            collective_id=0, has_side_effects=True, vmem_limit_bytes=46 * 2**20
        ),
        name="head_backward",
    )(hidden_state, norm_gain.reshape(1, feats), targets.reshape(4, 128), head_weight, gate_act, up_act)
    tiles = QUARTERS
    head_grad, down_grad, grad_hidden = pl.pallas_call(
        weights_kernel,
        grid=(tiles,),
        out_shape=(
            jax.ShapeDtypeStruct((feats, width), BF),
            jax.ShapeDtypeStruct((hidden_units, feats), BF),
            jax.ShapeDtypeStruct(hidden_state.shape, BF),
        ),
        in_specs=[vm] * 5 + [pl.BlockSpec((hidden_units // tiles, tokens), lambda i: (i, 0)), vm],
        out_specs=(
            pl.BlockSpec((feats, width // tiles), lambda i: (0, i)),
            pl.BlockSpec((hidden_units // tiles, feats), lambda i: (i, 0)),
            pl.BlockSpec(hidden_state.shape, lambda i: (0, 0)),
        ),
        compiler_params=pltpu.CompilerParams(vmem_limit_bytes=24 * 2**20),
        name="weight_gradients",
    )(scaled, *grads, act, resid.reshape(tokens, feats))
    return head_grad, grad_hidden, down_grad


def solution(mesh):
    in_specs = (P("col", "row"), P("row"), P("row", "col"), P(), P(None, "col"), P(None, "col"))
    out_specs = (P("row", "col"), P("col", "row"), P("col", "row"))
    return jax.shard_map(
        on_device, mesh=mesh, in_specs=in_specs, out_specs=out_specs, check_vma=False
    )
```
